256 devices in a mesh: group: 8 (over z_hi, x), prompts: 32 (over z_lo, y, core).
Axes of the slice: x: 4, y: 4, z: 8 (z_hi: 2, z_lo: 4; z = z_hi * 4 + z_lo), core: 2. Of those that a mesh axis runs over, the one named last changes fastest.
Arguments:
- queries: bfloat16 [32, 8, 256, 4096], P('prompts', 'group'), may hold values from -6 to 6
- resp_kv: bfloat16 [32, 8, 256, 2, 512], P('prompts', 'group'), may hold values from -6 to 6
- prefix_kv: bfloat16 [32, 8, 256, 2, 512], P('prompts', 'group'), may hold values from -6 to 6
- norm_gains: float32 [2, 128], replicated, may hold values from 0.25 to 1.75
- dout: bfloat16 [32, 8, 256, 4096], P('prompts', 'group'), may hold values from -48 to 48
- lengths: int32 [32, 8], P('prompts', 'group'), may hold values from 1 to 256, as said below
- rewards: int32 [32, 8], P('prompts', 'group'), may hold values from 0 to 3
- owner: int32 [32], P('prompts'), may hold values from 0 to 7
Outputs:
- d_queries: bfloat16 [32, 8, 256, 4096], P('prompts', 'group')
- d_resp_kv: bfloat16 [32, 8, 256, 2, 512], P('prompts', 'group')
- d_prefix_kv: bfloat16 [32, 8, 256, 2, 512], P('prompts', 'group')
- d_gains: float32 [2, 128], replicated
The draws below stay inside these ranges and needn't reach their ends.
Inputs may be any that keep to these rules, and one draw needn't show every extreme that they name: `lengths`: one response of the batch has exactly 256 live tokens.
All inputs are finite; a program needn't handle non-finite values.
Results may differ from the reference program's by a relative error of at most 0.012.
Values may be sent and summed in bfloat16 or wider, within the bound.
A program may use at most 64 MiB of HBM per device.

```python
from functools import partial
import jax
import jax.numpy as jnp
from jax import lax

HD = 128
QH = 32
KVH = 4
LEN = 256
PRE = 256
RESP = 8
PROMPTS = 32


def draw_lengths(key, part):
    key = jax.random.fold_in(key, 11)
    key_base, key_pick = jax.random.split(key, 2)
    uniform_lengths = jax.random.randint(key_base, (PROMPTS * RESP,), 1, LEN + 1)
    chosen = jax.random.randint(key_pick, (), 0, PROMPTS * RESP)
    flat_lengths = jnp.where(jnp.arange(PROMPTS * RESP) == chosen, LEN, uniform_lengths)
    return flat_lengths.reshape(PROMPTS, RESP).astype(jnp.int32)


def place_ends(values, own_key, low, largest):
    index_at = [jax.random.randint(jax.random.fold_in(own_key, axis), (), 0, length) for axis, length in enumerate(values.shape)]
    main_axis = values.shape.index(max(values.shape))
    neighbour = index_at[:main_axis] + [(index_at[main_axis] + 1) % values.shape[main_axis]] + index_at[main_axis + 1:]
    return values.at[tuple(index_at)].set(low).at[tuple(neighbour)].set(largest)


def levels(own_key, shape, shards, least, largest):
    def one(position, blocks):
        steps = jax.random.uniform(jax.random.fold_in(jax.random.fold_in(own_key, 6), position), (blocks,), jnp.float32, least / len(shards), largest / len(shards))
        return jnp.repeat(jnp.exp(steps), shape[position] // blocks).reshape((-1,) + (1,) * (len(shape) - position - 1))

    level = one(*shards[0])
    for cut in shards[1:]:
        level = level * one(*cut)
    return level


def centred(key, shape, scale, bound, cuts=(), held_as=jnp.bfloat16):
    values = jax.random.normal(key, shape, jnp.float32) * scale
    if len(cuts) > 0:
        values = levels(key, shape, cuts, -0.22, 0.18) * values
    return jnp.clip(values, min=-bound, max=bound).astype(held_as)


def setup_inputs(seed: int = 0) -> dict:
    key_of = jax.random.split(jax.random.key(seed), 9)
    return {
        "queries": centred(key_of[0], (PROMPTS, RESP, LEN, QH * HD), 1.0, 6.0, ((0, 32), (1, 8))),
        "resp_kv": centred(key_of[1], (PROMPTS, RESP, LEN, 2, KVH * HD), 1.0, 6.0, ((0, 32), (1, 8))),
        "prefix_kv": centred(key_of[2], (PROMPTS, RESP, PRE, 2, KVH * HD), 1.0, 6.0, ((0, 32), (1, 8))),
        "norm_gains": jnp.clip(1.0 + 0.15 * jax.random.normal(key_of[3], (2, HD), jnp.float32), 0.25, 1.75),
        "dout": centred(key_of[4], (PROMPTS, RESP, LEN, QH * HD), 8.0, 48.0, ((0, 32), (1, 8))),
        "lengths": draw_lengths(jax.random.fold_in(key_of[8], 71), 0),
        "rewards": place_ends(jax.random.randint(key_of[6], (PROMPTS, RESP), 0, 4), jax.random.fold_in(key_of[6], 1), 0, 3).astype(jnp.int32),
        "owner": place_ends(jax.random.randint(key_of[7], (PROMPTS,), 0, RESP), jax.random.fold_in(key_of[7], 1), 0, RESP - 1).astype(jnp.int32),
    }


EPSILON = 1e-06
THETA = 1000000.0

def rotate(values, cosine, sine_table):
    half_width = values.shape[-1] // 2
    lower_half = values[..., :half_width]
    upper_half = values[..., half_width:]
    return jnp.concatenate([lower_half * cosine - upper_half * sine_table, upper_half * cosine + lower_half * sine_table], -1)

def normalize(values, gain):
    return values * lax.rsqrt(lax.optimization_barrier(jnp.mean(values * values, -1, keepdims=True)) + EPSILON) * gain

def prepare(raw_queries, raw_keys, norm_gains, offset):
    tokens = raw_queries.shape[0]
    width = raw_queries.shape[-1]
    positions = offset + jnp.arange(tokens, dtype=jnp.float32)
    frequency = THETA ** (-2.0 * jnp.arange(width // 2, dtype=jnp.float32) / width)
    angles = positions[:, None] * frequency[None, :]
    cosine = jnp.cos(angles)[:, None, :]
    sine_table = jnp.sin(angles)[:, None, :]
    return (rotate(normalize(raw_queries, norm_gains[0]), cosine, sine_table), rotate(normalize(raw_keys, norm_gains[1]), cosine, sine_table))

def head_grads(head_queries, head_keys, head_values, head_cot):
    tokens = head_queries.shape[0]
    key_count = head_keys.shape[0]
    prefix_rows = key_count - tokens
    score_scale = head_queries.shape[-1] ** (-0.5)
    query_float = head_queries.astype(jnp.float32)
    key_float = head_keys.astype(jnp.float32)
    value_float = head_values.astype(jnp.float32)
    cot_float = head_cot.astype(jnp.float32)
    scores = jnp.einsum('tgd,sd->gts', query_float, key_float) * score_scale
    row_index = jnp.arange(tokens)[:, None]
    col_index = jnp.arange(key_count)[None, :]
    visible = (col_index < prefix_rows) | (col_index - prefix_rows <= row_index)
    exponents = jnp.where(visible[None], jnp.exp(scores), 0.0)
    weights = exponents / lax.optimization_barrier(jnp.sum(exponents, -1, keepdims=True))
    weights_b = weights.astype(jnp.bfloat16).astype(jnp.float32)
    outputs = jnp.einsum('gts,sd->gtd', weights_b, value_float)
    row_dots = jnp.einsum('tgd,gtd->gt', cot_float, outputs)
    prob_grad = jnp.einsum('tgd,sd->gts', cot_float, value_float)
    score_grad = (weights * (prob_grad - row_dots[..., None])).astype(jnp.bfloat16).astype(jnp.float32)
    query_grad = jnp.einsum('gts,sd->tgd', score_grad, key_float) * score_scale
    key_grad = jnp.einsum('gts,tgd->sd', score_grad, query_float) * score_scale
    value_grad = jnp.einsum('gts,tgd->sd', weights_b, cot_float)
    return (query_grad, key_grad, value_grad)

def response_grads(queries, resp_kv, prefix, norm_gains, dout, length, advantage):
    tokens = queries.shape[0]
    prefix_rows = prefix.shape[0]
    query_heads = queries.shape[1] // HD
    kv_heads = resp_kv.shape[2] // HD
    group_width = query_heads // kv_heads
    raw_queries = queries.astype(jnp.float32).reshape(tokens, query_heads, HD)
    raw_keys = resp_kv[:, 0].astype(jnp.float32).reshape(tokens, kv_heads, HD)
    (rotated_q, rotated_k), backward = jax.vjp(partial(prepare, offset=prefix_rows), raw_queries, raw_keys, norm_gains)
    query_b = rotated_q.astype(jnp.bfloat16)
    key_b = rotated_k.astype(jnp.bfloat16)
    live_rows = jnp.arange(tokens) < length
    cotangent = jnp.where(live_rows[:, None], dout.astype(jnp.float32) * advantage, 0.0)
    cotangent = cotangent.astype(jnp.bfloat16).reshape(tokens, query_heads, HD)
    resp_values = resp_kv[:, 1].reshape(tokens, kv_heads, HD)
    prefix_keys = prefix[:, 0].reshape(prefix_rows, kv_heads, HD)
    prefix_values = prefix[:, 1].reshape(prefix_rows, kv_heads, HD)
    query_parts = []
    key_parts = []
    value_parts = []
    for kv_head in range(kv_heads):
        first_head = kv_head * group_width
        head_keys = jnp.concatenate([prefix_keys[:, kv_head], key_b[:, kv_head]], 0)
        head_values = jnp.concatenate([prefix_values[:, kv_head], resp_values[:, kv_head]], 0)
        query_grad, key_grad, value_grad = head_grads(query_b[:, first_head:first_head + group_width], head_keys, head_values, cotangent[:, first_head:first_head + group_width])
        query_parts.append(query_grad)
        key_parts.append(key_grad)
        value_parts.append(value_grad)
    query_grads = jnp.concatenate(query_parts, 1)
    key_grads = jnp.stack(key_parts, 1)
    value_grads = jnp.stack(value_parts, 1)
    raw_query_grad, raw_key_grad, gain_grad = backward((query_grads, key_grads[prefix_rows:]))
    query_out = raw_query_grad.reshape(tokens, -1).astype(jnp.bfloat16)
    resp_out = jnp.stack([raw_key_grad.reshape(tokens, -1), value_grads[prefix_rows:].reshape(tokens, -1)], 1).astype(jnp.bfloat16)
    prefix_out = jnp.stack([key_grads[:prefix_rows].reshape(prefix_rows, -1), value_grads[:prefix_rows].reshape(prefix_rows, -1)], 1)
    return (query_out, resp_out, prefix_out, gain_grad)

def reference(queries, resp_kv, prefix_kv, norm_gains, dout, lengths, rewards, owner):
    group_size = rewards.shape[1]
    reward_values = rewards.astype(jnp.float32)
    mean_reward = lax.optimization_barrier(jnp.sum(reward_values, 1, keepdims=True)) / group_size
    square_mean = lax.optimization_barrier(jnp.sum(reward_values * reward_values, 1, keepdims=True)) / group_size
    spread = jnp.sqrt(jnp.maximum(square_mean - mean_reward * mean_reward, 0.0))
    advantages = (reward_values - mean_reward) / jnp.maximum(spread, 1.0)

    def per_prompt(inputs):
        prompt_q, prompt_kv, prompt_prefix, prompt_dout, prompt_len, prompt_adv, prompt_owner = inputs
        shared = lax.dynamic_index_in_dim(prompt_prefix, prompt_owner, 0, keepdims=False)

        def per_response(running, response_item):
            resp_q, item_kv, resp_dout, resp_len, resp_adv = response_item
            query_out, resp_out, prefix_out, gain_grad = response_grads(resp_q, item_kv, shared, norm_gains, resp_dout, resp_len, resp_adv)
            return ((running[0] + prefix_out, running[1] + gain_grad), (query_out, resp_out))
        start_sums = (jnp.zeros(shared.shape, jnp.float32), jnp.zeros(norm_gains.shape, jnp.float32))
        (prefix_sum, gain_sum), (query_outs, resp_outs) = lax.scan(per_response, start_sums, (prompt_q, prompt_kv, prompt_dout, prompt_len, prompt_adv))
        slot_mask = jnp.arange(group_size) == prompt_owner
        prefix_rounded = prefix_sum.astype(jnp.bfloat16)
        prefix_slots = jnp.where(slot_mask[:, None, None, None], prefix_rounded[None], jnp.zeros_like(prefix_rounded)[None])
        return (query_outs, resp_outs, prefix_slots, gain_sum)
    query_all, resp_all, prefix_all, gain_all = lax.map(per_prompt, (queries, resp_kv, prefix_kv, dout, lengths, advantages, owner))
    d_gains = lax.optimization_barrier(jnp.sum(gain_all, 0)) / (rewards.shape[0] * group_size)
    return (query_all, resp_all, prefix_all, d_gains)
```

```python
from functools import partial

import jax
import jax.numpy as jnp
import numpy as np
from jax import lax
from jax.experimental import pallas as pl
from jax.experimental.pallas import tpu as pltpu
from jax.sharding import PartitionSpec as P

HD = 128
T = 256
KVH = 4
GW = 8
NX = 4
CH = 64
EPSILON = 1e-06
THETA = 1000000.0
SCALE = HD**-0.5
LOG2E = 1.4426950408889634
LN2 = 0.6931471805599453
SHIFT = 40.0
UNROLL = 4
F32 = jnp.float32
BF = jnp.bfloat16
MESH = pl.DeviceIdType.MESH


def nn(a, b):
    return lax.dot_general(a, b, (((1,), (0,)), ((), ())), preferred_element_type=F32)


def nt(a, b):
    return lax.dot_general(a, b, (((1,), (1,)), ((), ())), preferred_element_type=F32)


def tables():
    positions = T + np.arange(T, dtype=np.float64)
    angles = positions[:, None] * (THETA ** (-2.0 * np.arange(HD // 2) / HD))[None, :]
    c, s = np.cos(angles), np.sin(angles)
    natural = np.stack([np.concatenate([c, c], 1), np.concatenate([-s, s], 1)])
    return natural.astype(np.float32), np.stack([c.T, s.T]).astype(np.float32)


def kernel(
    q_hbm, kv_hbm, px_hbm, gain_ref, do_hbm, len_ref, rew_ref, own_ref, nat_ref, tr_ref,
    dq_hbm, dkv_hbm, dpx_hbm, dg_ref,
    q_vm, do_vm, kv_vm, cot_vm, dq_vm, dkv_vm, dpx_vm,
    qn_s, qc_s, r_s, kall, vall, kt_s, kn_s, rk_s, tabs, amb, dka, dva, gacc, gks,
    e_s, p_s, wb_s, gb_s,
    a_buf, b_buf, c_buf, r_buf, rr_buf, t_buf, tt_buf, tf_buf, ff_buf,
    rw_buf, ga_buf, gb_buf, gc_buf,
    in_sem, out_sem, own_sem,
    p1_s, p1_r, bz_s, bz_r, ag_s, ag_r, rs_s, rs_r, rz_s, rz_r, fg_s, fg_r,
    rw_s, rw_r, ga_s, ga_r, gb2_s, gb2_r, gc_s, gc_r,
):
    me = lax.axis_index("group")
    pr = lax.axis_index("prompts")
    my_x, my_z = lax.rem(me, NX), lax.div(me, NX)
    my_yc, my_zl = lax.rem(pr, 8), lax.div(pr, 8)
    z_peer = {"group": lax.rem(me + NX, 2 * NX)}

    def x_peer(k):
        return {"group": my_z * NX + lax.rem(my_x + k, NX)}

    def g_peer(k):
        return {"group": lax.rem(me + k, 2 * NX)}

    def yc_peer(k):
        return {"prompts": my_zl * 8 + lax.rem(my_yc + k, 8)}

    def zl_peer(k):
        return {"prompts": lax.rem(my_zl + k, 4) * 8 + my_yc}

    def behind(mine, k, n):
        return lax.rem(mine + n - k, n)

    def remote(src, dst, ss, rs, dev):
        return pltpu.make_async_remote_copy(
            src_ref=src, dst_ref=dst, send_sem=ss, recv_sem=rs, device_id=dev, device_id_type=MESH
        )

    barrier = pltpu.get_barrier_semaphore()
    for k in range(1, 8):
        pl.semaphore_signal(barrier, inc=1, device_id=g_peer(k), device_id_type=MESH)
        pl.semaphore_signal(barrier, inc=1, device_id=yc_peer(k), device_id_type=MESH)
    for k in range(1, 4):
        pl.semaphore_signal(barrier, inc=1, device_id=zl_peer(k), device_id_type=MESH)

    def in_copy(kind, g):
        cols = pl.ds(pl.multiple_of(g * (GW * HD), GW * HD), GW * HD)
        src, dst = ((q_hbm, q_vm), (do_hbm, do_vm))[kind]
        return pltpu.make_async_copy(src.at[:, cols], dst.at[:, cols], in_sem.at[kind, g])

    def out_copy(g):
        cols = pl.ds(pl.multiple_of(g * (GW * HD), GW * HD), GW * HD)
        return pltpu.make_async_copy(dq_vm.at[:, cols], dq_hbm.at[:, cols], out_sem.at[g])

    kv_copy = pltpu.make_async_copy(kv_hbm, kv_vm, in_sem.at[2, 0])
    kv_copy.start()
    for g in range(KVH):
        in_copy(0, g).start()
        in_copy(1, g).start()

    rw_buf[me] = jnp.full((8, HD), rew_ref[0, 0].astype(F32), F32)
    gain_t = jnp.broadcast_to(gain_ref[0:1, :], (HD, HD)).T
    gain_t = jnp.concatenate([gain_t, gain_t], 1)
    cos_c, sin_c = tr_ref[0] * (SCALE * LOG2E), tr_ref[1] * (SCALE * LOG2E)
    tabs[0] = gain_t[:64] * cos_c
    tabs[1] = gain_t[64:] * sin_c
    tabs[2] = gain_t[64:] * cos_c
    tabs[3] = gain_t[:64] * sin_c
    gacc[...] = jnp.zeros_like(gacc)
    gks[...] = jnp.zeros_like(gks)
    gk = gain_ref[1:2, :]
    tri = lax.broadcasted_iota(jnp.int32, (HD, HD), 0) <= lax.broadcasted_iota(jnp.int32, (HD, HD), 1)
    owner = own_ref[0]
    owner_x, owner_z = lax.rem(owner, NX), lax.div(owner, NX)

    pl.semaphore_wait(barrier, 17)

    def head_cols(g):
        return pl.ds(pl.multiple_of(g * HD, HD), HD)

    def rows(x):
        return pl.ds(pl.multiple_of(x * CH, CH), CH)

    def rw_copy(k, slot):
        return remote(rw_buf.at[me], rw_buf.at[slot], rw_s.at[k], rw_r.at[k], g_peer(k))

    for k in range(1, 8):
        rw_copy(k, me).start()

    def p1_copy(g, k, slot):
        src = px_hbm.at[rows(lax.rem(my_x + k, NX)), :, head_cols(g)]
        return remote(src, a_buf[g].at[slot], p1_s.at[g, k], p1_r.at[g, k], x_peer(k))

    def own_copy(g):
        return pltpu.make_async_copy(px_hbm.at[rows(my_x), :, head_cols(g)], a_buf[g].at[my_x], own_sem.at[g])

    def bz_copy(g, slot):
        return remote(b_buf[g].at[my_z], b_buf[g].at[slot], bz_s.at[g], bz_r.at[g], z_peer)

    def ag_copy(g, k, x):
        return remote(c_buf.at[g, rows(my_x)], c_buf.at[g, rows(x)], ag_s.at[g, k], ag_r.at[g, k], x_peer(k))

    for g in range(KVH):
        for k in range(1, NX):
            p1_copy(g, k, my_x).start()
        own_copy(g).start()

    def bc1(g):
        own_copy(g).wait()
        for k in range(1, NX):
            p1_copy(g, k, behind(my_x, k, NX)).wait_recv()
        b_buf[g][my_z] = a_buf[g][owner_x]
        bz_copy(g, my_z).start()

    def bc2(g):
        bz_copy(g, 1 - my_z).wait_recv()
        c_buf[g, rows(my_x)] = b_buf[g][owner_z]
        for k in range(1, NX):
            ag_copy(g, k, my_x).start()

    def bc3(g):
        for k in range(1, NX):
            ag_copy(g, k, behind(my_x, k, NX)).wait_recv()
        kall[g, 0:T] = c_buf[g, :, 0, :]
        vall[g, 0:T] = c_buf[g, :, 1, :]
        kt_s[g] = kall[g].T

    def rs_copy(g, k, slot):
        src = r_buf.at[g, rows(lax.rem(my_x + k, NX))]
        return remote(src, rr_buf.at[g, slot], rs_s.at[g, k], rs_r.at[g, k], x_peer(k))

    def rz_copy(g):
        return remote(t_buf.at[g], tt_buf.at[g], rz_s.at[g], rz_r.at[g], z_peer)

    def fg_copy(g, k, x):
        return remote(ff_buf.at[g, rows(my_x)], ff_buf.at[g, rows(x)], fg_s.at[g, k], fg_r.at[g, k], x_peer(k))

    def rd1(g):
        r_buf[g, :, 0:HD] = (dka[0:T] * LN2).astype(BF)
        r_buf[g, :, HD:] = dva[0:T].astype(BF)
        tf_buf[g, :, 0:HD] = dka[rows(my_x)] * LN2
        tf_buf[g, :, HD:] = dva[rows(my_x)]
        for k in range(1, NX):
            rs_copy(g, k, my_x).start()

    def rd2(g):
        total = tf_buf[g]
        for k in range(1, NX):
            rs_copy(g, k, behind(my_x, k, NX)).wait_recv()
            total = total + rr_buf[g, behind(my_x, k, NX)].astype(F32)
        tf_buf[g] = total
        t_buf[g] = total.astype(BF)
        rz_copy(g).start()

    def rd3(g):
        rz_copy(g).wait_recv()
        ff_buf[g, rows(my_x)] = (tf_buf[g] + tt_buf[g].astype(F32)).astype(BF)
        for k in range(1, NX):
            fg_copy(g, k, my_x).start()

    def rd4(g):
        for k in range(1, NX):
            fg_copy(g, k, behind(my_x, k, NX)).wait_recv()
        mine = owner == me
        cols = head_cols(g)
        dpx_vm[:, 0, cols] = jnp.where(mine, ff_buf[g, :, 0:HD], jnp.zeros((T, HD), BF))
        dpx_vm[:, 1, cols] = jnp.where(mine, ff_buf[g, :, HD:], jnp.zeros((T, HD), BF))

    kv_copy.wait()

    def key_prep(g, _):
        cols = head_cols(g)
        raw = kv_vm[:, 0, cols].astype(F32)
        rk = lax.rsqrt(jnp.mean(raw * raw, -1, keepdims=True) + EPSILON)
        kn = raw * rk
        kn_s[g] = kn
        rk_s[g] = jnp.broadcast_to(rk, (T, HD))
        kg = kn * gk
        kall[g, T : 2 * T] = (kg * nat_ref[0] + pltpu.roll(kg, HD // 2, 1) * nat_ref[1]).astype(BF)
        vall[g, T : 2 * T] = kv_vm[:, 1, cols]
        return 0

    lax.fori_loop(0, KVH, key_prep, 0)

    for k in range(1, 8):
        rw_copy(k, behind(me, k, 8)).wait_recv()
    total = rw_buf[0]
    square = rw_buf[0] * rw_buf[0]
    for k in range(1, 8):
        total = total + rw_buf[k]
        square = square + rw_buf[k] * rw_buf[k]
    mean = total / 8
    spread = jnp.sqrt(jnp.maximum(square / 8 - mean * mean, 0.0))
    advantage = (rw_buf[me] - mean) / jnp.maximum(spread, 1.0)
    live = lax.broadcasted_iota(jnp.int32, (T, HD), 0) < len_ref[0, 0]
    amb[...] = jnp.where(live, jnp.broadcast_to(advantage[0:1, :], (T, HD)), 0.0)

    def query_prep(g):
        in_copy(0, g).wait()
        in_copy(1, g).wait()

        def one(h):
            cols = head_cols(h)
            cot_vm[:, cols] = (do_vm[:, cols].astype(F32) * amb[...]).astype(BF)
            x = q_vm[:, cols].T.astype(F32)
            r = lax.rsqrt(jnp.sum(x * x, 0, keepdims=True) * (1.0 / HD) + EPSILON)
            qn = x * r
            qa, qb = qn[:64], qn[64:]
            r_s[h] = jnp.broadcast_to(r, (8, T))
            qn_s[h] = qn
            qc_s[h, 0:64] = (qa * tabs[0] - qb * tabs[1]).astype(BF)
            qc_s[h, 64:HD] = (qb * tabs[2] + qa * tabs[3]).astype(BF)

        def some(i, _):
            for j in range(UNROLL):
                one(g * GW + i * UNROLL + j)
            return 0

        lax.fori_loop(0, GW // UNROLL, some, 0)

    query_prep(0)
    bc1(0)
    query_prep(1)
    bc1(1)
    bc2(0)
    query_prep(2)
    bc1(2)
    bc2(1)
    query_prep(3)
    bc1(3)
    bc2(2)
    bc2(3)

    def head(g, h, slot):
        cols = head_cols(h)
        cot = cot_vm[:, cols]
        qc = qc_s[h]
        e_r, p_r, wb_r, gb_r = e_s.at[slot], p_s.at[slot], wb_s.at[slot], gb_s.at[slot]
        sum_e = jnp.zeros((8, T), F32)
        sum_ep = jnp.zeros((8, T), F32)
        for s0 in range(0, 2 * T, HD):
            block = slice(s0, s0 + HD)
            scores = nn(kall[g, block], qc)
            prob = nt(vall[g, block], cot)
            e = jnp.exp2(scores - SHIFT)
            if s0 == T:
                e = jnp.concatenate([jnp.where(tri, e[:, :HD], 0.0), e[:, HD:]], 1)
            elif s0 == T + HD:
                e = jnp.concatenate([jnp.zeros((HD, HD), F32), jnp.where(tri, e[:, HD:], 0.0)], 1)
            e_r[block] = e
            p_r[block] = prob
            sum_e = sum_e + jnp.sum(e.reshape(HD // 8, 8, T), 0)
            sum_ep = sum_ep + jnp.sum((e * prob).reshape(HD // 8, 8, T), 0)
        inv = 1.0 / jnp.sum(sum_e, 0, keepdims=True)
        dots = jnp.sum(sum_ep, 0, keepdims=True) * inv
        for s0 in range(0, 2 * T, HD):
            block = slice(s0, s0 + HD)
            w = e_r[block] * inv
            wb_r[block] = w.astype(BF)
            gb_r[block] = (w * (p_r[block] - dots)).astype(BF)
        dva[...] += nn(wb_r[...], cot)
        dka[...] += nt(gb_r[...], qc)
        dt = nn(kt_s[g], gb_r[...])
        da, db = dt[:64], dt[64:]
        va = da * tabs[0] + db * tabs[3]
        vb = db * tabs[2] - da * tabs[1]
        qa, qb = qn_s[h, 0:64], qn_s[h, 64:HD]
        pa, pb = va * qa, vb * qb
        gacc[0:64] += pa
        gacc[64:HD] += pb
        m = (jnp.sum(pa, 0, keepdims=True) + jnp.sum(pb, 0, keepdims=True)) * (1.0 / HD)
        r = r_s[h, 0:1] * LN2
        dx = jnp.concatenate([(va - qa * m) * r, (vb - qb * m) * r], 0).astype(BF)
        dq_vm[:, cols] = dx.T

    def key_head(g, _):
        bc3(g)
        dka[...] = jnp.zeros_like(dka)
        dva[...] = jnp.zeros_like(dva)

        def some(i, _):
            for j in range(UNROLL):
                head(g, g * GW + i * UNROLL + j, j)

            @pl.when((g > 0) & (i == 0))
            def _():
                rd2(g - 1)

            @pl.when((g > 0) & (i == 1))
            def _():
                rd3(g - 1)

            return 0

        lax.fori_loop(0, GW // UNROLL, some, 0)
        rd1(g)
        out_copy(g).start()
        cols = head_cols(g)
        dk = dka[T : 2 * T] * LN2
        u = dk * nat_ref[0] - pltpu.roll(dk, HD // 2, 1) * nat_ref[1]
        kn = kn_s[g]
        gks[0:1] += jnp.sum(u * kn, 0, keepdims=True)
        v = u * gk
        m = jnp.mean(v * kn, -1, keepdims=True)
        dkv_vm[:, 0, cols] = (rk_s[g] * (v - kn * m)).astype(BF)
        dkv_vm[:, 1, cols] = dva[T : 2 * T].astype(BF)
        return 0

    lax.fori_loop(0, KVH, key_head, 0)

    def stage(buf, mine, n, peer, ss, rs):
        def copy(k, slot):
            return remote(buf.at[mine], buf.at[slot], ss.at[k], rs.at[k], peer(k))

        def start():
            for k in range(1, n):
                copy(k, mine).start()

        def finish():
            for k in range(1, n):
                copy(k, behind(mine, k, n)).wait_recv()
            out = buf[0]
            for k in range(1, n):
                out = out + buf[k]
            return out

        def drain():
            for k in range(1, n):
                copy(k, mine).wait_send()

        return start, finish, drain

    ga_start, ga_finish, ga_drain = stage(ga_buf, me, 8, g_peer, ga_s, ga_r)
    gb_start, gb_finish, gb_drain = stage(gb_buf, my_yc, 8, yc_peer, gb2_s, gb2_r)
    gc_start, gc_finish, gc_drain = stage(gc_buf, my_zl, 4, zl_peer, gc_s, gc_r)

    dkv_copy = pltpu.make_async_copy(dkv_vm, dkv_hbm, out_sem.at[4])
    dkv_copy.start()
    gq = jnp.broadcast_to(jnp.sum(gacc[...], 1, keepdims=True), (HD, HD)).T * LN2 / gain_ref[0:1, :]
    ga_buf[me] = jnp.concatenate([gq[0:1], gks[0:1], jnp.zeros((6, HD), F32)], 0)
    ga_start()
    rd2(KVH - 1)
    gb_buf[my_yc] = ga_finish()
    gb_start()
    rd3(KVH - 1)
    gc_buf[my_zl] = gb_finish()
    gc_start()
    for g in range(KVH):
        rd4(g)
    dpx_copy = pltpu.make_async_copy(dpx_vm, dpx_hbm, out_sem.at[5])
    dpx_copy.start()
    dg_ref[...] = gc_finish()[0:2] * (1.0 / 256)

    for k in range(1, 8):
        rw_copy(k, me).wait_send()
    ga_drain()
    gb_drain()
    gc_drain()
    for g in range(KVH):
        bz_copy(g, my_z).wait_send()
        rz_copy(g).wait_send()
        for k in range(1, NX):
            p1_copy(g, k, my_x).wait_send()
            ag_copy(g, k, my_x).wait_send()
            rs_copy(g, k, my_x).wait_send()
            fg_copy(g, k, my_x).wait_send()
        out_copy(g).wait()
    dkv_copy.wait()
    dpx_copy.wait()


def body(queries, resp_kv, prefix_kv, norm_gains, dout, lengths, rewards, owner):
    natural, transposed = tables()
    anywhere = pl.BlockSpec(memory_space=pl.ANY)
    vmem = pl.BlockSpec(memory_space=pltpu.VMEM)
    smem = pl.BlockSpec(memory_space=pltpu.SMEM)
    dma = pltpu.SemaphoreType.DMA
    out = pl.pallas_call(
        kernel,
        out_shape=[
            jax.ShapeDtypeStruct((T, 4096), BF),
            jax.ShapeDtypeStruct((T, 2, 512), BF),
            jax.ShapeDtypeStruct((T, 2, 512), BF),
            jax.ShapeDtypeStruct((2, HD), F32),
        ],
        in_specs=[anywhere, anywhere, anywhere, vmem, anywhere, smem, smem, smem, vmem, vmem],
        out_specs=[anywhere, anywhere, anywhere, vmem],
        scratch_shapes=[
            pltpu.VMEM((T, 4096), BF),
            pltpu.VMEM((T, 4096), BF),
            pltpu.VMEM((T, 2, 512), BF),
            pltpu.VMEM((T, 4096), BF),
            pltpu.VMEM((T, 4096), BF),
            pltpu.VMEM((T, 2, 512), BF),
            pltpu.VMEM((T, 2, 512), BF),
            pltpu.VMEM((32, HD, T), F32),
            pltpu.VMEM((32, HD, T), BF),
            pltpu.VMEM((32, 8, T), F32),
            pltpu.VMEM((KVH, 2 * T, HD), BF),
            pltpu.VMEM((KVH, 2 * T, HD), BF),
            pltpu.VMEM((KVH, HD, 2 * T), BF),
            pltpu.VMEM((KVH, T, HD), F32),
            pltpu.VMEM((KVH, T, HD), F32),
            pltpu.VMEM((4, HD // 2, T), F32),
            pltpu.VMEM((T, HD), F32),
            pltpu.VMEM((2 * T, HD), F32),
            pltpu.VMEM((2 * T, HD), F32),
            pltpu.VMEM((HD, T), F32),
            pltpu.VMEM((8, HD), F32),
            pltpu.VMEM((UNROLL, 2 * T, T), F32),
            pltpu.VMEM((UNROLL, 2 * T, T), F32),
            pltpu.VMEM((UNROLL, 2 * T, T), BF),
            pltpu.VMEM((UNROLL, 2 * T, T), BF),
            [pltpu.VMEM((NX, CH, 2, HD), BF)] * KVH,
            [pltpu.VMEM((2, CH, 2, HD), BF)] * KVH,
            pltpu.VMEM((KVH, T, 2, HD), BF),
            pltpu.VMEM((KVH, T, 2 * HD), BF),
            pltpu.VMEM((KVH, NX, CH, 2 * HD), BF),
            pltpu.VMEM((KVH, CH, 2 * HD), BF),
            pltpu.VMEM((KVH, CH, 2 * HD), BF),
            pltpu.VMEM((KVH, CH, 2 * HD), F32),
            pltpu.VMEM((KVH, T, 2 * HD), BF),
            pltpu.VMEM((8, 8, HD), F32),
            pltpu.VMEM((8, 8, HD), F32),
            pltpu.VMEM((8, 8, HD), F32),
            pltpu.VMEM((4, 8, HD), F32),
            dma((3, KVH)),
            dma((6,)),
            dma((KVH,)),
            dma((KVH, NX)),
            dma((KVH, NX)),
            dma((KVH,)),
            dma((KVH,)),
            dma((KVH, NX)),
            dma((KVH, NX)),
            dma((KVH, NX)),
            dma((KVH, NX)),
            dma((KVH,)),
            dma((KVH,)),
            dma((KVH, NX)),
            dma((KVH, NX)),
            dma((8,)),
            dma((8,)),
            dma((8,)),
            dma((8,)),
            dma((8,)),
            dma((8,)),
            dma((4,)),
            dma((4,)),
        ],
        compiler_params=pltpu.CompilerParams(
            collective_id=0, has_side_effects=True, vmem_limit_bytes=48 << 20
        ),
    )(
        queries[0, 0], resp_kv[0, 0], prefix_kv[0, 0], norm_gains, dout[0, 0],
        lengths, rewards, owner, natural, transposed,
    )
    return (out[0][None, None], out[1][None, None], out[2][None, None], out[3])


def solution(mesh):
    return jax.shard_map(
        body,
        mesh=mesh,
        in_specs=(
            P("prompts", "group", None, None),
            P("prompts", "group", None, None, None),
            P("prompts", "group", None, None, None),
            P(),
            P("prompts", "group", None, None),
            P("prompts", "group"),
            P("prompts", "group"),
            P("prompts"),
        ),
        out_specs=(
            P("prompts", "group", None, None),
            P("prompts", "group", None, None, None),
            P("prompts", "group", None, None, None),
            P(),
        ),
        check_vma=False,
    )
```

```python
from functools import partial

import jax
import jax.numpy as jnp
import numpy as np
from jax import lax
from jax.experimental import pallas as pl
from jax.experimental.pallas import tpu as pltpu
from jax.sharding import PartitionSpec as P

HD = 128
T = 256
KVH = 4
GW = 8
NX = 4
CH = 64
EPSILON = 1e-06
THETA = 1000000.0
SCALE = HD**-0.5
LOG2E = 1.4426950408889634
LN2 = 0.6931471805599453
SHIFT = 40.0
UNROLL = 4
F32 = jnp.float32
BF = jnp.bfloat16
MESH = pl.DeviceIdType.MESH


def nn(a, b):
    return lax.dot_general(a, b, (((1,), (0,)), ((), ())), preferred_element_type=F32)


def nt(a, b):
    return lax.dot_general(a, b, (((1,), (1,)), ((), ())), preferred_element_type=F32)


def tables():
    positions = T + np.arange(T, dtype=np.float64)
    angles = positions[:, None] * (THETA ** (-2.0 * np.arange(HD // 2) / HD))[None, :]
    c, s = np.cos(angles), np.sin(angles)
    natural = np.stack([np.concatenate([c, c], 1), np.concatenate([-s, s], 1)])
    return natural.astype(np.float32), np.stack([c.T, s.T]).astype(np.float32)


def kernel(
    q_hbm, kv_hbm, px_hbm, gain_hbm, do_hbm, len_hbm, rew_hbm, own_hbm, nat_hbm, tr_hbm,
    dq_hbm, dkv_hbm, dpx_hbm, dg_ref,
    gain_ref, nat_ref, tr_ref, len_ref, rew_ref, own_ref,
    q_vm, do_vm, kv_vm, dkv_vm, dpx_vm,
    qn_s, qc_s, r_s, er_s, pr_s, se_s, sp_s, wr_s, kall, vall, kt_s, kn_s, rk_s, tabs, mask_s, adv_s,
    dkp, dkr, dva, gacc, gks,
    e_s, p_s, wb_s, gb_s,
    a_buf, b_buf, c_buf, r_buf, rr_buf, t_buf, tt_buf, tf_buf, ff_buf,
    rw_buf, ga_buf, gb_buf,
    in_sem, small_sem, out_sem, own_sem,
    p1_s, p1_r, bz_s, bz_r, ag_s, ag_r, rs_s, rs_r, rz_s, rz_r, fg_s, fg_r,
    rw_s, rw_r, ga_s, ga_r, gb2_s, gb2_r,
):
    me = lax.axis_index("group")
    pr = lax.axis_index("prompts")
    my_x, my_z = lax.rem(me, NX), lax.div(me, NX)
    my_core, my_y, my_zl = lax.rem(pr, 2), lax.rem(lax.div(pr, 2), 4), lax.div(pr, 8)
    my_a = my_x * 4 + my_y
    my_b = (my_z * 4 + my_zl) * 2 + my_core
    z_peer = {"group": lax.rem(me + NX, 2 * NX), "prompts": pr}

    def x_peer(k):
        return {"group": my_z * NX + lax.rem(my_x + k, NX), "prompts": pr}

    def g_peer(k):
        return {"group": lax.rem(me + k, 2 * NX), "prompts": pr}

    def a_peer(k):
        a = lax.rem(my_a + k, 16)
        return {"group": my_z * 4 + lax.div(a, 4), "prompts": (my_zl * 4 + lax.rem(a, 4)) * 2 + my_core}

    def b_peer(k):
        b = lax.rem(my_b + k, 16)
        z = lax.div(b, 2)
        return {"group": lax.div(z, 4) * 4 + my_x, "prompts": (lax.rem(z, 4) * 4 + my_y) * 2 + lax.rem(b, 2)}

    def behind(mine, k, n):
        return lax.rem(mine + n - k, n)

    def remote(src, dst, ss, rs, dev):
        return pltpu.make_async_remote_copy(
            src_ref=src, dst_ref=dst, send_sem=ss, recv_sem=rs, device_id=dev, device_id_type=MESH
        )

    def greet(dev):
        pl.semaphore_signal(barrier, inc=1, device_id=dev, device_id_type=MESH)

    barrier = pltpu.get_barrier_semaphore()
    for k in range(1, 16):
        greet(b_peer(k))
        greet(a_peer(k))
    for k in range(1, NX):
        greet({"group": (1 - my_z) * NX + lax.rem(my_x + k, NX), "prompts": pr})

    small = (
        (kv_hbm, kv_vm), (nat_hbm, nat_ref), (tr_hbm, tr_ref), (gain_hbm, gain_ref),
        (len_hbm, len_ref), (rew_hbm, rew_ref), (own_hbm, own_ref),
    )
    small_copies = [pltpu.make_async_copy(a, b, small_sem.at[i]) for i, (a, b) in enumerate(small)]

    def wide(g):
        return pl.ds(pl.multiple_of(g * (GW * HD), GW * HD), GW * HD)

    def in_copy(kind, g):
        src, dst = ((q_hbm, q_vm), (do_hbm, do_vm))[kind]
        return pltpu.make_async_copy(src.at[:, wide(g)], dst.at[:, wide(g)], in_sem.at[kind, g])

    def out_copy(g):
        return pltpu.make_async_copy(q_vm.at[:, wide(g)], dq_hbm.at[:, wide(g)], out_sem.at[g])

    for copy in small_copies:
        copy.start()
    for g in range(KVH):
        in_copy(0, g).start()
        in_copy(1, g).start()
    for copy in small_copies:
        copy.wait()

    rw_buf[me] = jnp.full((8, HD), rew_ref[0, 0].astype(F32), F32)
    gain_t = jnp.broadcast_to(gain_ref[0:1, :], (HD, HD)).T
    gain_t = jnp.concatenate([gain_t, gain_t], 1)
    cos_c, sin_c = tr_ref[0] * (SCALE * LOG2E), tr_ref[1] * (SCALE * LOG2E)
    tabs[0] = gain_t[:64] * cos_c
    tabs[1] = gain_t[64:] * sin_c
    tabs[2] = gain_t[64:] * cos_c
    tabs[3] = gain_t[:64] * sin_c
    gacc[...] = jnp.zeros_like(gacc)
    gks[...] = jnp.zeros_like(gks)
    gk = gain_ref[1:2, :]
    mask_s[...] = jnp.where(lax.broadcasted_iota(jnp.int32, (8, T), 1) < len_ref[0, 0], 1.0, 0.0)
    tri = lax.broadcasted_iota(jnp.int32, (HD, HD), 0) <= lax.broadcasted_iota(jnp.int32, (HD, HD), 1)
    owner = own_ref[0]
    owner_x, owner_z = lax.rem(owner, NX), lax.div(owner, NX)

    def head_cols(g):
        return pl.ds(pl.multiple_of(g * HD, HD), HD)

    def rows(x):
        return pl.ds(pl.multiple_of(x * CH, CH), CH)

    def rw_copy(k, slot):
        return remote(rw_buf.at[me], rw_buf.at[slot], rw_s.at[k], rw_r.at[k], g_peer(k))

    def p1_copy(g, k, slot):
        src = px_hbm.at[rows(lax.rem(my_x + k, NX)), :, head_cols(g)]
        return remote(src, a_buf[g].at[slot], p1_s.at[g, k], p1_r.at[g, k], x_peer(k))

    def own_copy(g):
        return pltpu.make_async_copy(px_hbm.at[rows(my_x), :, head_cols(g)], a_buf[g].at[my_x], own_sem.at[g])

    def bz_copy(g, slot):
        return remote(b_buf[g].at[my_z], b_buf[g].at[slot], bz_s.at[g], bz_r.at[g], z_peer)

    def ag_copy(g, k, x):
        return remote(c_buf.at[g, rows(my_x)], c_buf.at[g, rows(x)], ag_s.at[g, k], ag_r.at[g, k], x_peer(k))

    def bc1(g):
        own_copy(g).wait()
        for k in range(1, NX):
            p1_copy(g, k, behind(my_x, k, NX)).wait_recv()
        b_buf[g][my_z] = a_buf[g][owner_x]
        bz_copy(g, my_z).start()

    def bc2(g):
        bz_copy(g, 1 - my_z).wait_recv()
        c_buf[g, rows(my_x)] = b_buf[g][owner_z]
        for k in range(1, NX):
            ag_copy(g, k, my_x).start()

    def bc3(g):
        for k in range(1, NX):
            ag_copy(g, k, behind(my_x, k, NX)).wait_recv()
        kall[g, 0:T] = c_buf[g, :, 0, :]
        vall[g, 0:T] = c_buf[g, :, 1, :]
        kt_s[g] = kall[g].T

    def rs_copy(g, k, slot):
        src = r_buf.at[g, rows(lax.rem(my_x + k, NX))]
        return remote(src, rr_buf.at[g, slot], rs_s.at[g, k], rs_r.at[g, k], x_peer(k))

    def rz_copy(g):
        return remote(t_buf.at[g], tt_buf.at[g], rz_s.at[g], rz_r.at[g], z_peer)

    def fg_copy(g, k, x):
        return remote(ff_buf.at[g, rows(my_x)], ff_buf.at[g, rows(x)], fg_s.at[g, k], fg_r.at[g, k], x_peer(k))

    def rd1(g):
        adv = adv_s[0:1, 0:HD]
        r_buf[g, :, 0:HD] = (dkp[...] * (adv * LN2)).astype(BF)
        r_buf[g, :, HD:] = (dva[...] * adv).astype(BF)
        for k in range(1, NX):
            rs_copy(g, k, my_x).start()
        tf_buf[g, :, 0:HD] = dkp[rows(my_x)] * (adv * LN2)
        tf_buf[g, :, HD:] = dva[rows(my_x)] * adv

    def rd2(g):
        total = tf_buf[g]
        for k in range(1, NX):
            rs_copy(g, k, behind(my_x, k, NX)).wait_recv()
            total = total + rr_buf[g, behind(my_x, k, NX)].astype(F32)
        tf_buf[g] = total
        t_buf[g] = total.astype(BF)
        rz_copy(g).start()

    def rd3(g):
        rz_copy(g).wait_recv()
        ff_buf[g, rows(my_x)] = (tf_buf[g] + tt_buf[g].astype(F32)).astype(BF)
        for k in range(1, NX):
            fg_copy(g, k, my_x).start()

    def rd4(g):
        for k in range(1, NX):
            fg_copy(g, k, behind(my_x, k, NX)).wait_recv()
        mine = owner == me
        cols = head_cols(g)
        dpx_vm[:, 0, cols] = jnp.where(mine, ff_buf[g, :, 0:HD], jnp.zeros((T, HD), BF))
        dpx_vm[:, 1, cols] = jnp.where(mine, ff_buf[g, :, HD:], jnp.zeros((T, HD), BF))

    def key_prep(g, _):
        cols = head_cols(g)
        raw = kv_vm[:, 0, cols].astype(F32)
        rk = lax.rsqrt(jnp.mean(raw * raw, -1, keepdims=True) + EPSILON)
        kn = raw * rk
        kn_s[g] = kn
        rk_s[g] = jnp.broadcast_to(rk, (T, HD))
        kg = kn * gk
        kall[g, T : 2 * T] = (kg * nat_ref[0] + pltpu.roll(kg, HD // 2, 1) * nat_ref[1]).astype(BF)
        vall[g, T : 2 * T] = kv_vm[:, 1, cols]
        return 0

    lax.fori_loop(0, KVH, key_prep, 0)

    def first_part(g, h):
        cols = head_cols(h)
        cot = do_vm[:, cols]
        x = q_vm[:, cols].T.astype(F32)
        r = lax.rsqrt(jnp.sum(x * x, 0, keepdims=True) * (1.0 / HD) + EPSILON)
        qn = x * r
        qa, qb = qn[:64], qn[64:]
        r_s[h] = jnp.broadcast_to(r, (8, T))
        qn_s[h] = qn
        qc = jnp.concatenate([qa * tabs[0] - qb * tabs[1], qb * tabs[2] + qa * tabs[3]], 0).astype(BF)
        qc_s[h] = qc
        sum_e = jnp.zeros((8, T), F32)
        sum_ep = jnp.zeros((8, T), F32)
        for s0 in range(0, T, HD):
            scores = nn(kall[g, T + s0 : T + s0 + HD], qc)
            prob = nt(vall[g, T + s0 : T + s0 + HD], cot)
            e = jnp.exp2(scores - SHIFT)
            if s0 == 0:
                e = jnp.concatenate([jnp.where(tri, e[:, :HD], 0.0), e[:, HD:]], 1)
            else:
                e = jnp.concatenate([jnp.zeros((HD, HD), F32), jnp.where(tri, e[:, HD:], 0.0)], 1)
            er_s[h, s0 : s0 + HD] = e
            pr_s[h, s0 : s0 + HD] = prob
            sum_e = sum_e + jnp.sum(e.reshape(HD // 8, 8, T), 0)
            sum_ep = sum_ep + jnp.sum((e * prob).reshape(HD // 8, 8, T), 0)
        se_s[h] = sum_e
        sp_s[h] = sum_ep

    steps = KVH * GW // UNROLL
    per = GW // UNROLL

    def when(i, at):
        return pl.when(i == at * per - 1)

    def first_parts(i, _):
        g = lax.div(i, per)

        @pl.when(lax.rem(i, per) == 0)
        def _():
            in_copy(0, g).wait()
            in_copy(1, g).wait()

        for j in range(UNROLL):
            first_part(g, i * UNROLL + j)

        @when(i, 1)
        def _():
            pl.semaphore_wait(barrier, 33)
            for g in range(KVH):
                for k in range(1, NX):
                    p1_copy(g, k, my_x).start()
                own_copy(g).start()
            for k in range(1, 8):
                rw_copy(k, me).start()

        return 0

    lax.fori_loop(0, steps, first_parts, 0)
    for g in range(KVH):
        bc1(g)

    for k in range(1, 8):
        rw_copy(k, behind(me, k, 8)).wait_recv()
    total = rw_buf[0]
    square = rw_buf[0] * rw_buf[0]
    for k in range(1, 8):
        total = total + rw_buf[k]
        square = square + rw_buf[k] * rw_buf[k]
    mean = total / 8
    spread = jnp.sqrt(jnp.maximum(square / 8 - mean * mean, 0.0))
    advantage = (rw_buf[me] - mean) / jnp.maximum(spread, 1.0)
    adv_s[...] = jnp.concatenate([advantage, advantage], 1)
    for g in range(KVH):
        bc2(g)

    def second_part(g, h, slot):
        cols = head_cols(h)
        cot = do_vm[:, cols]
        qc = qc_s[h]
        e_r, p_r, wb_r = e_s.at[slot], p_s.at[slot], wb_s.at[slot]
        sum_e = se_s[h]
        sum_ep = sp_s[h]
        for s0 in range(0, T, HD):
            block = slice(s0, s0 + HD)
            scores = nn(kall[g, block], qc)
            prob = nt(vall[g, block], cot)
            e = jnp.exp2(scores - SHIFT)
            e_r[block] = e
            p_r[block] = prob
            sum_e = sum_e + jnp.sum(e.reshape(HD // 8, 8, T), 0)
            sum_ep = sum_ep + jnp.sum((e * prob).reshape(HD // 8, 8, T), 0)
        inv = mask_s[0:1] / jnp.sum(sum_e, 0, keepdims=True)
        dots = jnp.sum(sum_ep, 0, keepdims=True) * inv
        se_s[h] = jnp.broadcast_to(inv, (8, T))
        sp_s[h] = jnp.broadcast_to(dots, (8, T))
        for s0 in range(0, T, HD):
            block = slice(s0, s0 + HD)
            w = e_r[block] * inv
            wb_r[block] = w.astype(BF)
            gb_s[h, block] = (w * (p_r[block] - dots)).astype(BF)
        dva[...] += nn(wb_r[...], cot)
        dkp[...] += nt(gb_s[h, 0:T], qc)

    def second_parts(i, _):
        g = lax.div(i, per)

        @pl.when(lax.rem(i, per) == 0)
        def _():
            bc3(g)
            dkp[...] = jnp.zeros_like(dkp)
            dva[...] = jnp.zeros_like(dva)

        for j in range(UNROLL):
            second_part(g, i * UNROLL + j, j)

        @pl.when(lax.rem(i, per) == per - 1)
        def _():
            rd1(g)

        @when(i, 3)
        def _():
            rd2(0)

        @when(i, 4)
        def _():
            rd2(1)

        return 0

    lax.fori_loop(0, steps, second_parts, 0)

    def third_part(g, h):
        cols = head_cols(h)
        inv = se_s[h, 0:1]
        dots = sp_s[h, 0:1]
        for s0 in range(0, T, HD):
            w = er_s[h, s0 : s0 + HD] * inv
            wr_s[h, s0 : s0 + HD] = w.astype(BF)
            gb_s[h, T + s0 : T + s0 + HD] = (w * (pr_s[h, s0 : s0 + HD] - dots)).astype(BF)
        dkr[...] += nt(gb_s[h, T : 2 * T], qc_s[h])
        dt = nn(kt_s[g], gb_s[h])
        da, db = dt[:64], dt[64:]
        va = da * tabs[0] + db * tabs[3]
        vb = db * tabs[2] - da * tabs[1]
        qa, qb = qn_s[h, 0:64], qn_s[h, 64:HD]
        pa, pb = va * qa, vb * qb
        gacc[0:64] += pa
        gacc[64:HD] += pb
        m = (jnp.sum(pa, 0, keepdims=True) + jnp.sum(pb, 0, keepdims=True)) * (1.0 / HD)
        r = r_s[h, 0:1] * (adv_s[0:1] * LN2)
        dx = jnp.concatenate([(va - qa * m) * r, (vb - qb * m) * r], 0).astype(BF)
        q_vm[:, cols] = dx.T

    def key_grads(g):
        dk = dkr[...] * LN2
        u = dk * nat_ref[0] - pltpu.roll(dk, HD // 2, 1) * nat_ref[1]
        kn = kn_s[g]
        gks[0:1] += jnp.sum(u * kn, 0, keepdims=True)
        v = u * gk
        m = jnp.mean(v * kn, -1, keepdims=True)
        dkv_vm[:, 0, head_cols(g)] = (rk_s[g] * adv_s[0:1, 0:HD] * (v - kn * m)).astype(BF)

    def third_parts(i, _):
        g = lax.div(i, per)

        @pl.when(lax.rem(i, per) == 0)
        def _():
            dkr[...] = jnp.zeros_like(dkr)

        for j in range(UNROLL):
            third_part(g, i * UNROLL + j)

        @pl.when(lax.rem(i, per) == per - 1)
        def _():
            key_grads(g)
            out_copy(g).start()

        @when(i, 1)
        def _():
            rd2(2)
            rd3(0)

        @when(i, 2)
        def _():
            rd2(3)
            rd3(1)

        @when(i, 3)
        def _():
            rd3(2)
            rd4(0)

        return 0

    lax.fori_loop(0, steps, third_parts, 0)
    last = KVH - 1

    def stage(buf, mine, peer, ss, rs):
        def copy(k, slot):
            return remote(buf.at[mine], buf.at[slot], ss.at[k], rs.at[k], peer(k))

        def start():
            for k in range(1, 16):
                copy(k, mine).start()

        def finish():
            for k in range(1, 16):
                copy(k, behind(mine, k, 16)).wait_recv()
            out = buf[0]
            for k in range(1, 16):
                out = out + buf[k]
            return out

        def drain():
            for k in range(1, 16):
                copy(k, mine).wait_send()

        return start, finish, drain

    ga_start, ga_finish, ga_drain = stage(ga_buf, my_a, a_peer, ga_s, ga_r)
    gb_start, gb_finish, gb_drain = stage(gb_buf, my_b, b_peer, gb2_s, gb2_r)

    gq = jnp.broadcast_to(jnp.sum(gacc[...], 1, keepdims=True), (HD, HD)).T * LN2 / gain_ref[0:1, :]
    ga_buf[my_a] = jnp.concatenate([gq[0:1], gks[0:1], jnp.zeros((6, HD), F32)], 0) * adv_s[:, 0:HD]
    ga_start()

    def value_grads(g, _):
        total = jnp.zeros((T, HD), F32)
        for j in range(GW):
            h = g * GW + j
            total = total + nn(wr_s[h], do_vm[:, head_cols(h)])
        dkv_vm[:, 1, head_cols(g)] = (total * adv_s[0:1, 0:HD]).astype(BF)
        return 0

    rd3(last)
    lax.fori_loop(0, KVH, value_grads, 0)
    rd4(1)
    gb_buf[my_b] = ga_finish()
    gb_start()
    dkv_copy = pltpu.make_async_copy(dkv_vm, dkv_hbm, out_sem.at[4])
    dkv_copy.start()
    rd4(2)
    for k in range(1, 8):
        rw_copy(k, me).wait_send()
    ga_drain()
    for g in range(KVH):
        bz_copy(g, my_z).wait_send()
        rz_copy(g).wait_send()
        for k in range(1, NX):
            p1_copy(g, k, my_x).wait_send()
            ag_copy(g, k, my_x).wait_send()
            rs_copy(g, k, my_x).wait_send()
        out_copy(g).wait()
    rd4(last)
    dpx_copy = pltpu.make_async_copy(dpx_vm, dpx_hbm, out_sem.at[5])
    dpx_copy.start()
    dg_ref[...] = gb_finish()[0:2] * (1.0 / 256)
    gb_drain()
    for g in range(KVH):
        for k in range(1, NX):
            fg_copy(g, k, my_x).wait_send()
    dkv_copy.wait()
    dpx_copy.wait()


def body(queries, resp_kv, prefix_kv, norm_gains, dout, lengths, rewards, owner):
    natural, transposed = tables()
    anywhere = pl.BlockSpec(memory_space=pl.ANY)
    vmem = pl.BlockSpec(memory_space=pltpu.VMEM)
    dma = pltpu.SemaphoreType.DMA
    heads = KVH * GW
    out = pl.pallas_call(
        kernel,
        out_shape=[
            jax.ShapeDtypeStruct((T, 4096), BF),
            jax.ShapeDtypeStruct((T, 2, 512), BF),
            jax.ShapeDtypeStruct((T, 2, 512), BF),
            jax.ShapeDtypeStruct((2, HD), F32),
        ],
        in_specs=[anywhere] * 10,
        out_specs=[anywhere, anywhere, anywhere, vmem],
        scratch_shapes=[
            pltpu.VMEM((2, HD), F32),
            pltpu.VMEM((2, T, HD), F32),
            pltpu.VMEM((2, HD // 2, T), F32),
            pltpu.SMEM((1, 1), jnp.int32),
            pltpu.SMEM((1, 1), jnp.int32),
            pltpu.SMEM((1,), jnp.int32),
            pltpu.VMEM((T, 4096), BF),
            pltpu.VMEM((T, 4096), BF),
            pltpu.VMEM((T, 2, 512), BF),
            pltpu.VMEM((T, 2, 512), BF),
            pltpu.VMEM((T, 2, 512), BF),
            pltpu.VMEM((heads, HD, T), F32),
            pltpu.VMEM((heads, HD, T), BF),
            pltpu.VMEM((heads, 8, T), F32),
            pltpu.VMEM((heads, T, T), F32),
            pltpu.VMEM((heads, T, T), F32),
            pltpu.VMEM((heads, 8, T), F32),
            pltpu.VMEM((heads, 8, T), F32),
            pltpu.VMEM((heads, T, T), BF),
            pltpu.VMEM((KVH, 2 * T, HD), BF),
            pltpu.VMEM((KVH, 2 * T, HD), BF),
            pltpu.VMEM((KVH, HD, 2 * T), BF),
            pltpu.VMEM((KVH, T, HD), F32),
            pltpu.VMEM((KVH, T, HD), F32),
            pltpu.VMEM((4, HD // 2, T), F32),
            pltpu.VMEM((8, T), F32),
            pltpu.VMEM((8, T), F32),
            pltpu.VMEM((T, HD), F32),
            pltpu.VMEM((T, HD), F32),
            pltpu.VMEM((T, HD), F32),
            pltpu.VMEM((HD, T), F32),
            pltpu.VMEM((8, HD), F32),
            pltpu.VMEM((UNROLL, T, T), F32),
            pltpu.VMEM((UNROLL, T, T), F32),
            pltpu.VMEM((UNROLL, T, T), BF),
            pltpu.VMEM((heads, 2 * T, T), BF),
            [pltpu.VMEM((NX, CH, 2, HD), BF)] * KVH,
            [pltpu.VMEM((2, CH, 2, HD), BF)] * KVH,
            pltpu.VMEM((KVH, T, 2, HD), BF),
            pltpu.VMEM((KVH, T, 2 * HD), BF),
            pltpu.VMEM((KVH, NX, CH, 2 * HD), BF),
            pltpu.VMEM((KVH, CH, 2 * HD), BF),
            pltpu.VMEM((KVH, CH, 2 * HD), BF),
            pltpu.VMEM((KVH, CH, 2 * HD), F32),
            pltpu.VMEM((KVH, T, 2 * HD), BF),
            pltpu.VMEM((8, 8, HD), F32),
            pltpu.VMEM((16, 8, HD), F32),
            pltpu.VMEM((16, 8, HD), F32),
            dma((2, KVH)),
            dma((7,)),
            dma((6,)),
            dma((KVH,)),
            dma((KVH, NX)),
            dma((KVH, NX)),
            dma((KVH,)),
            dma((KVH,)),
            dma((KVH, NX)),
            dma((KVH, NX)),
            dma((KVH, NX)),
            dma((KVH, NX)),
            dma((KVH,)),
            dma((KVH,)),
            dma((KVH, NX)),
            dma((KVH, NX)),
            dma((8,)),
            dma((8,)),
            dma((16,)),
            dma((16,)),
            dma((16,)),
            dma((16,)),
        ],
        compiler_params=pltpu.CompilerParams(
            collective_id=0, has_side_effects=True, vmem_limit_bytes=56 << 20
        ),
    )(
        queries[0, 0], resp_kv[0, 0], prefix_kv[0, 0], norm_gains, dout[0, 0],
        lengths, rewards, owner, natural, transposed,
    )
    return (out[0][None, None], out[1][None, None], out[2][None, None], out[3])


def solution(mesh):
    return jax.shard_map(
        body,
        mesh=mesh,
        in_specs=(
            P("prompts", "group", None, None),
            P("prompts", "group", None, None, None),
            P("prompts", "group", None, None, None),
            P(),
            P("prompts", "group", None, None),
            P("prompts", "group"),
            P("prompts", "group"),
            P("prompts"),
        ),
        out_specs=(
            P("prompts", "group", None, None),
            P("prompts", "group", None, None, None),
            P("prompts", "group", None, None, None),
            P(),
        ),
        check_vma=False,
    )
```

```python
from functools import partial

import jax
import jax.numpy as jnp
import numpy as np
from jax import lax
from jax.experimental import pallas as pl
from jax.experimental.pallas import tpu as pltpu
from jax.sharding import PartitionSpec as P

HD = 128
T = 256
KVH = 4
GW = 8
NX = 4
CH = 64
EPSILON = 1e-06
THETA = 1000000.0
SCALE = HD**-0.5
LOG2E = 1.4426950408889634
LN2 = 0.6931471805599453
SHIFT = 40.0
F32 = jnp.float32
BF = jnp.bfloat16
MESH = pl.DeviceIdType.MESH


def nn(a, b):
    return lax.dot_general(a, b, (((1,), (0,)), ((), ())), preferred_element_type=F32)


def nt(a, b):
    return lax.dot_general(a, b, (((1,), (1,)), ((), ())), preferred_element_type=F32)


def tables():
    positions = T + np.arange(T, dtype=np.float64)
    angles = positions[:, None] * (THETA ** (-2.0 * np.arange(HD // 2) / HD))[None, :]
    c, s = np.cos(angles), np.sin(angles)
    natural = np.stack([np.concatenate([c, c], 1), np.concatenate([-s, s], 1)])
    return natural.astype(np.float32), np.stack([c.T, s.T]).astype(np.float32)


def kernel(
    q_hbm, kv_hbm, px_hbm, gain_hbm, do_hbm, len_hbm, rew_hbm, own_hbm, nat_hbm, tr_hbm,
    dq_hbm, dkv_hbm, dpx_hbm, dg_ref,
    gain_ref, nat_ref, tr_ref, len_ref, rew_ref, own_ref,
    q_vm, do_vm, kv_vm, dkv_vm, dpx_vm,
    qn_s, qc_s, r_s, er_s, pr_s, se_s, sp_s, wr_s, kall, vall, kt_s, kn_s, rk_s, tabs, mask_s, adv_s,
    dkp, dkr, dva, gacc, gks,
    e_s, p_s, wb_s, gb_s,
    a_buf, b_buf, c_buf, r_buf, rr_buf, t_buf, tt_buf, tf_buf, ff_buf,
    rw_buf, ga_buf, gb_buf,
    in_sem, small_sem, out_sem, own_sem, px_sem,
    p1_s, p1_r, bz_s, bz_r, ag_s, ag_r, rs_s, rs_r, rz_s, rz_r, fg_s, fg_r,
    rw_s, rw_r, ga_s, ga_r, gb2_s, gb2_r,
):
    me = lax.axis_index("group")
    pr = lax.axis_index("prompts")
    my_x, my_z = lax.rem(me, NX), lax.div(me, NX)
    my_core, my_y, my_zl = lax.rem(pr, 2), lax.rem(lax.div(pr, 2), 4), lax.div(pr, 8)
    my_a = my_x * 4 + my_y
    my_b = (my_z * 4 + my_zl) * 2 + my_core
    z_peer = {"group": lax.rem(me + NX, 2 * NX), "prompts": pr}

    def x_peer(k):
        return {"group": my_z * NX + lax.rem(my_x + k, NX), "prompts": pr}

    def g_peer(k):
        return {"group": lax.rem(me + k, 2 * NX), "prompts": pr}

    def a_peer(k):
        a = lax.rem(my_a + k, 16)
        return {"group": my_z * 4 + lax.div(a, 4), "prompts": (my_zl * 4 + lax.rem(a, 4)) * 2 + my_core}

    def b_peer(k):
        b = lax.rem(my_b + k, 16)
        z = lax.div(b, 2)
        return {"group": lax.div(z, 4) * 4 + my_x, "prompts": (lax.rem(z, 4) * 4 + my_y) * 2 + lax.rem(b, 2)}

    def behind(mine, k, n):
        return lax.rem(mine + n - k, n)

    def remote(src, dst, ss, rs, dev):
        return pltpu.make_async_remote_copy(
            src_ref=src, dst_ref=dst, send_sem=ss, recv_sem=rs, device_id=dev, device_id_type=MESH
        )

    def greet(dev):
        pl.semaphore_signal(barrier, inc=1, device_id=dev, device_id_type=MESH)

    barrier = pltpu.get_barrier_semaphore()
    for k in range(15, 0, -1):
        greet(b_peer(k))
    for k in range(1, 16):
        greet(a_peer(k))
    for k in range(1, NX):
        greet({"group": (1 - my_z) * NX + lax.rem(my_x + k, NX), "prompts": pr})

    small = (
        (kv_hbm, kv_vm), (nat_hbm, nat_ref), (tr_hbm, tr_ref), (gain_hbm, gain_ref),
        (len_hbm, len_ref), (rew_hbm, rew_ref), (own_hbm, own_ref),
    )
    small_copies = [pltpu.make_async_copy(a, b, small_sem.at[i]) for i, (a, b) in enumerate(small)]

    def wide(g):
        return pl.ds(pl.multiple_of(g * (GW * HD), GW * HD), GW * HD)

    def in_copy(kind, g):
        src, dst = ((q_hbm, q_vm), (do_hbm, do_vm))[kind]
        return pltpu.make_async_copy(src.at[:, wide(g)], dst.at[:, wide(g)], in_sem.at[kind, g])

    def out_copy(g):
        return pltpu.make_async_copy(q_vm.at[:, wide(g)], dq_hbm.at[:, wide(g)], out_sem.at[g])

    def head_cols(g):
        return pl.ds(pl.multiple_of(g * HD, HD), HD)

    def rows(x):
        return pl.ds(pl.multiple_of(x * CH, CH), CH)

    def p1_copy(g, k, slot):
        src = px_hbm.at[rows(lax.rem(my_x + k, NX)), :, head_cols(g)]
        return remote(src, a_buf[g].at[slot], p1_s.at[g, k], p1_r.at[g, k], x_peer(k))

    def own_copy(g):
        return pltpu.make_async_copy(px_hbm.at[rows(my_x), :, head_cols(g)], a_buf[g].at[my_x], own_sem.at[g])

    for copy in small_copies:
        copy.start()
    for g in range(KVH):
        own_copy(g).start()
        in_copy(0, g).start()
        in_copy(1, g).start()
    for copy in small_copies:
        copy.wait()

    rw_buf[me] = jnp.full((8, HD), rew_ref[0, 0].astype(F32), F32)
    gain_t = jnp.broadcast_to(gain_ref[0:1, :], (HD, HD)).T
    gain_t = jnp.concatenate([gain_t, gain_t], 1)
    cos_c, sin_c = tr_ref[0] * (SCALE * LOG2E), tr_ref[1] * (SCALE * LOG2E)
    tabs[0] = gain_t[:64] * cos_c
    tabs[1] = gain_t[64:] * sin_c
    tabs[2] = gain_t[64:] * cos_c
    tabs[3] = gain_t[:64] * sin_c
    gacc[...] = jnp.zeros_like(gacc)
    gks[...] = jnp.zeros_like(gks)
    gk = gain_ref[1:2, :]
    mask_s[...] = jnp.where(lax.broadcasted_iota(jnp.int32, (8, T), 1) < len_ref[0, 0], 1.0, 0.0)
    tri = lax.broadcasted_iota(jnp.int32, (HD, HD), 0) <= lax.broadcasted_iota(jnp.int32, (HD, HD), 1)
    owner = own_ref[0]
    owner_x, owner_z = lax.rem(owner, NX), lax.div(owner, NX)

    def rw_copy(k, slot):
        return remote(rw_buf.at[me], rw_buf.at[slot], rw_s.at[k], rw_r.at[k], g_peer(k))


    def bz_copy(g, slot):
        return remote(b_buf[g].at[my_z], b_buf[g].at[slot], bz_s.at[g], bz_r.at[g], z_peer)

    def ag_copy(g, k, x):
        return remote(c_buf.at[g, rows(my_x)], c_buf.at[g, rows(x)], ag_s.at[g, k], ag_r.at[g, k], x_peer(k))

    def bc1(g):
        own_copy(g).wait()
        for k in range(1, NX):
            p1_copy(g, k, behind(my_x, k, NX)).wait_recv()
        b_buf[g][my_z] = a_buf[g][owner_x]
        bz_copy(g, my_z).start()

    def bc2(g):
        bz_copy(g, 1 - my_z).wait_recv()
        c_buf[g, rows(my_x)] = b_buf[g][owner_z]
        for k in range(1, NX):
            ag_copy(g, k, my_x).start()

    def bc3(g):
        for k in range(1, NX):
            ag_copy(g, k, behind(my_x, k, NX)).wait_recv()
        kall[g, 0:T] = c_buf[g, :, 0, :]
        vall[g, 0:T] = c_buf[g, :, 1, :]
        kt_s[g] = kall[g].T

    def rs_copy(g, k, slot):
        src = r_buf.at[g, rows(lax.rem(my_x + k, NX))]
        return remote(src, rr_buf.at[g, slot], rs_s.at[g, k], rs_r.at[g, k], x_peer(k))

    def rz_copy(g):
        return remote(t_buf.at[g], tt_buf.at[g], rz_s.at[g], rz_r.at[g], z_peer)

    def fg_copy(g, k, x):
        return remote(ff_buf.at[g, rows(my_x)], ff_buf.at[g, rows(x)], fg_s.at[g, k], fg_r.at[g, k], x_peer(k))

    def rd1(g):
        adv = adv_s[0:1, 0:HD]
        r_buf[g, :, 0:HD] = (dkp[...] * (adv * LN2)).astype(BF)
        r_buf[g, :, HD:] = (dva[...] * adv).astype(BF)
        for k in range(1, NX):
            rs_copy(g, k, my_x).start()
        tf_buf[g, :, 0:HD] = dkp[rows(my_x)] * (adv * LN2)
        tf_buf[g, :, HD:] = dva[rows(my_x)] * adv

    def rd2(g):
        total = tf_buf[g]
        for k in range(1, NX):
            rs_copy(g, k, behind(my_x, k, NX)).wait_recv()
            total = total + rr_buf[g, behind(my_x, k, NX)].astype(F32)
        tf_buf[g] = total
        t_buf[g] = total.astype(BF)
        rz_copy(g).start()

    def rd3(g):
        rz_copy(g).wait_recv()
        ff_buf[g, rows(my_x)] = (tf_buf[g] + tt_buf[g].astype(F32)).astype(BF)
        for k in range(1, NX):
            fg_copy(g, k, my_x).start()

    def dpx_copy(g):
        cols = head_cols(g)
        return pltpu.make_async_copy(dpx_vm.at[:, :, cols], dpx_hbm.at[:, :, cols], px_sem.at[g])

    def rd4(g):
        for k in range(1, NX):
            fg_copy(g, k, behind(my_x, k, NX)).wait_recv()
        mine = owner == me
        cols = head_cols(g)
        dpx_vm[:, 0, cols] = jnp.where(mine, ff_buf[g, :, 0:HD], jnp.zeros((T, HD), BF))
        dpx_vm[:, 1, cols] = jnp.where(mine, ff_buf[g, :, HD:], jnp.zeros((T, HD), BF))
        dpx_copy(g).start()

    def key_prep(g, _):
        cols = head_cols(g)
        raw = kv_vm[:, 0, cols].astype(F32)
        rk = lax.rsqrt(jnp.mean(raw * raw, -1, keepdims=True) + EPSILON)
        kn = raw * rk
        kn_s[g] = kn
        rk_s[g] = jnp.broadcast_to(rk, (T, HD))
        kg = kn * gk
        kall[g, T : 2 * T] = (kg * nat_ref[0] + pltpu.roll(kg, HD // 2, 1) * nat_ref[1]).astype(BF)
        vall[g, T : 2 * T] = kv_vm[:, 1, cols]
        return 0

    lax.fori_loop(0, KVH, key_prep, 0)

    pl.semaphore_wait(barrier, 33)
    for g in range(KVH):
        for k in range(1, NX):
            p1_copy(g, k, my_x).start()
    for k in range(1, 8):
        rw_copy(k, me).start()

    def lanes(j):
        return slice(j * T, j * T + T)

    def cots(g):
        return jnp.concatenate([do_vm[:, head_cols(g * GW + j)] for j in range(GW)], 0)

    def first_part(g, j):
        h = g * GW + j
        cols = head_cols(h)
        cot = do_vm[:, cols]
        x = q_vm[:, cols].T.astype(F32)
        r = lax.rsqrt(jnp.sum(x * x, 0, keepdims=True) * (1.0 / HD) + EPSILON)
        qn = x * r
        qa, qb = qn[:64], qn[64:]
        r_s[h] = jnp.broadcast_to(r, (8, T))
        qn_s[h] = qn
        qc = jnp.concatenate([qa * tabs[0] - qb * tabs[1], qb * tabs[2] + qa * tabs[3]], 0).astype(BF)
        qc_s[g, :, lanes(j)] = qc
        sum_e = jnp.zeros((8, T), F32)
        sum_ep = jnp.zeros((8, T), F32)
        for s0 in range(0, T, HD):
            scores = nn(kall[g, T + s0 : T + s0 + HD], qc)
            prob = nt(vall[g, T + s0 : T + s0 + HD], cot)
            e = jnp.exp2(scores - SHIFT)
            if s0 == 0:
                e = jnp.concatenate([jnp.where(tri, e[:, :HD], 0.0), e[:, HD:]], 1)
            else:
                e = jnp.concatenate([jnp.zeros((HD, HD), F32), jnp.where(tri, e[:, HD:], 0.0)], 1)
            er_s[h, s0 : s0 + HD] = e
            pr_s[h, s0 : s0 + HD] = prob
            sum_e = sum_e + jnp.sum(e.reshape(HD // 8, 8, T), 0)
            sum_ep = sum_ep + jnp.sum((e * prob).reshape(HD // 8, 8, T), 0)
        se_s[h] = sum_e
        sp_s[h] = sum_ep

    def first_parts(g, _):
        in_copy(0, g).wait()
        in_copy(1, g).wait()
        for j in range(GW):
            first_part(g, j)

        @pl.when(g == 2)
        def _():
            bc1(0)
            bc1(1)

        @pl.when(g == 3)
        def _():
            bc1(2)
            bc1(3)

        return 0

    lax.fori_loop(0, KVH, first_parts, 0)

    for g in range(KVH):
        bc2(g)

    for k in range(1, 8):
        rw_copy(k, behind(me, k, 8)).wait_recv()
    total = rw_buf[0]
    square = rw_buf[0] * rw_buf[0]
    for k in range(1, 8):
        total = total + rw_buf[k]
        square = square + rw_buf[k] * rw_buf[k]
    mean = total / 8
    spread = jnp.sqrt(jnp.maximum(square / 8 - mean * mean, 0.0))
    advantage = (rw_buf[me] - mean) / jnp.maximum(spread, 1.0)
    adv_s[...] = jnp.concatenate([advantage, advantage], 1)

    def second_part(g, j):
        h = g * GW + j
        cols = head_cols(h)
        cot = do_vm[:, cols]
        qc = qc_s[g, :, lanes(j)]
        e_r, p_r = e_s.at[j], p_s.at[j]
        sum_e = se_s[h]
        sum_ep = sp_s[h]
        for s0 in range(0, T, HD):
            block = slice(s0, s0 + HD)
            scores = nn(kall[g, block], qc)
            prob = nt(vall[g, block], cot)
            e = jnp.exp2(scores - SHIFT)
            e_r[block] = e
            p_r[block] = prob
            sum_e = sum_e + jnp.sum(e.reshape(HD // 8, 8, T), 0)
            sum_ep = sum_ep + jnp.sum((e * prob).reshape(HD // 8, 8, T), 0)
        inv = mask_s[0:1] / jnp.sum(sum_e, 0, keepdims=True)
        dots = jnp.sum(sum_ep, 0, keepdims=True) * inv
        se_s[h] = jnp.broadcast_to(inv, (8, T))
        sp_s[h] = jnp.broadcast_to(dots, (8, T))
        for s0 in range(0, T, HD):
            block = slice(s0, s0 + HD)
            w = e_r[block] * inv
            wb_s[block, lanes(j)] = w.astype(BF)
            gb_s[g, block, lanes(j)] = (w * (p_r[block] - dots)).astype(BF)

    def second_parts(g, _):
        bc3(g)
        for j in range(GW):
            second_part(g, j)
        dva[...] = nn(wb_s[...], cots(g))
        dkp[...] = nt(gb_s[g, 0:T], qc_s[g])
        rd1(g)

        @pl.when(g == 3)
        def _():
            rd2(0)

        return 0

    lax.fori_loop(0, KVH, second_parts, 0)

    def third_part(g, j):
        h = g * GW + j
        cols = head_cols(h)
        inv = se_s[h, 0:1]
        dots = sp_s[h, 0:1]
        for s0 in range(0, T, HD):
            w = er_s[h, s0 : s0 + HD] * inv
            wr_s[g, s0 : s0 + HD, lanes(j)] = w.astype(BF)
            gb_s[g, T + s0 : T + s0 + HD, lanes(j)] = (w * (pr_s[h, s0 : s0 + HD] - dots)).astype(BF)
        dt = nn(kt_s[g], gb_s[g, :, lanes(j)])
        da, db = dt[:64], dt[64:]
        va = da * tabs[0] + db * tabs[3]
        vb = db * tabs[2] - da * tabs[1]
        qa, qb = qn_s[h, 0:64], qn_s[h, 64:HD]
        pa, pb = va * qa, vb * qb
        gacc[0:64] += pa
        gacc[64:HD] += pb
        m = (jnp.sum(pa, 0, keepdims=True) + jnp.sum(pb, 0, keepdims=True)) * (1.0 / HD)
        r = r_s[h, 0:1] * (adv_s[0:1] * LN2)
        dx = jnp.concatenate([(va - qa * m) * r, (vb - qb * m) * r], 0).astype(BF)
        q_vm[:, cols] = dx.T

    def key_grads(g):
        dk = dkr[...] * LN2
        u = dk * nat_ref[0] - pltpu.roll(dk, HD // 2, 1) * nat_ref[1]
        kn = kn_s[g]
        gks[0:1] += jnp.sum(u * kn, 0, keepdims=True)
        v = u * gk
        m = jnp.mean(v * kn, -1, keepdims=True)
        dkv_vm[:, 0, head_cols(g)] = (rk_s[g] * adv_s[0:1, 0:HD] * (v - kn * m)).astype(BF)

    def third_parts(g, _):
        for j in range(GW):
            third_part(g, j)
        dkr[...] = nt(gb_s[g, T : 2 * T], qc_s[g])
        key_grads(g)
        out_copy(g).start()

        @pl.when(g == 0)
        def _():
            rd2(1)

        @pl.when(g == 1)
        def _():
            rd2(2)

        @pl.when(g == 2)
        def _():
            rd2(3)

        return 0

    lax.fori_loop(0, KVH, third_parts, 0)
    last = KVH - 1

    def stage(buf, mine, peer, ss, rs):
        def copy(k, slot):
            return remote(buf.at[mine], buf.at[slot], ss.at[k], rs.at[k], peer(k))

        def start():
            for k in range(1, 16):
                copy(k, mine).start()

        def finish():
            for k in range(1, 16):
                copy(k, behind(mine, k, 16)).wait_recv()
            out = buf[0]
            for k in range(1, 16):
                out = out + buf[k]
            return out

        def drain():
            for k in range(1, 16):
                copy(k, mine).wait_send()

        return start, finish, drain

    ga_start, ga_finish, ga_drain = stage(ga_buf, my_a, a_peer, ga_s, ga_r)
    gb_start, gb_finish, gb_drain = stage(gb_buf, my_b, b_peer, gb2_s, gb2_r)

    gq = jnp.broadcast_to(jnp.sum(gacc[...], 1, keepdims=True), (HD, HD)).T * LN2 / gain_ref[0:1, :]
    ga_buf[my_a] = jnp.concatenate([gq[0:1], gks[0:1], jnp.zeros((6, HD), F32)], 0) * adv_s[:, 0:HD]
    ga_start()
    rd3(0)

    def value_grads(g, _):
        total = nn(wr_s[g], cots(g))
        dkv_vm[:, 1, head_cols(g)] = (total * adv_s[0:1, 0:HD]).astype(BF)
        return 0

    lax.fori_loop(0, KVH, value_grads, 0)
    dkv_copy = pltpu.make_async_copy(dkv_vm, dkv_hbm, out_sem.at[4])
    dkv_copy.start()
    rd3(1)
    rd3(2)
    rd3(last)
    gb_buf[my_b] = ga_finish()
    gb_start()
    rd4(0)
    rd4(1)
    rd4(2)
    for k in range(1, 8):
        rw_copy(k, me).wait_send()
    ga_drain()
    for g in range(KVH):
        bz_copy(g, my_z).wait_send()
        rz_copy(g).wait_send()
        for k in range(1, NX):
            p1_copy(g, k, my_x).wait_send()
            ag_copy(g, k, my_x).wait_send()
            rs_copy(g, k, my_x).wait_send()
        out_copy(g).wait()
    dkv_copy.wait()
    rd4(last)
    dg_ref[...] = gb_finish()[0:2] * (1.0 / 256)
    gb_drain()
    for g in range(KVH):
        for k in range(1, NX):
            fg_copy(g, k, my_x).wait_send()
        dpx_copy(g).wait()


def finish(*refs):
    sources, results, held, in_sem, out_sem = refs[:4], refs[4:8], refs[8:12], refs[12], refs[13]
    parts = [(0, pl.ds(i * 64, 64)) for i in range(4)] + [(1, pl.ds(0, T)), (2, pl.ds(0, T)), (3, pl.ds(0, 2))]
    arrive = [pltpu.make_async_copy(sources[a].at[p], held[a].at[p], in_sem.at[i]) for i, (a, p) in enumerate(parts)]
    leave = [pltpu.make_async_copy(held[a].at[p], results[a].at[p], out_sem.at[i]) for i, (a, p) in enumerate(parts)]
    for copy in arrive:
        copy.start()
    for came, goes in zip(arrive, leave):
        came.wait()
        goes.start()
    for copy in leave:
        copy.wait()


def body(queries, resp_kv, prefix_kv, norm_gains, dout, lengths, rewards, owner):
    natural, transposed = tables()
    anywhere = pl.BlockSpec(memory_space=pl.ANY)
    vmem = pl.BlockSpec(memory_space=pltpu.VMEM)
    dma = pltpu.SemaphoreType.DMA
    heads = KVH * GW
    shapes = [
        jax.ShapeDtypeStruct((T, 4096), BF),
        jax.ShapeDtypeStruct((T, 2, 512), BF),
        jax.ShapeDtypeStruct((T, 2, 512), BF),
        jax.ShapeDtypeStruct((2, HD), F32),
    ]
    out = pl.pallas_call(
        kernel,
        out_shape=shapes,
        in_specs=[anywhere] * 10,
        out_specs=[anywhere, anywhere, anywhere, vmem],
        scratch_shapes=[
            pltpu.VMEM((2, HD), F32),
            pltpu.VMEM((2, T, HD), F32),
            pltpu.VMEM((2, HD // 2, T), F32),
            pltpu.SMEM((1, 1), jnp.int32),
            pltpu.SMEM((1, 1), jnp.int32),
            pltpu.SMEM((1,), jnp.int32),
            pltpu.VMEM((T, 4096), BF),
            pltpu.VMEM((T, 4096), BF),
            pltpu.VMEM((T, 2, 512), BF),
            pltpu.VMEM((T, 2, 512), BF),
            pltpu.VMEM((T, 2, 512), BF),
            pltpu.VMEM((heads, HD, T), F32),
            pltpu.VMEM((KVH, HD, GW * T), BF),
            pltpu.VMEM((heads, 8, T), F32),
            pltpu.VMEM((heads, T, T), F32),
            pltpu.VMEM((heads, T, T), F32),
            pltpu.VMEM((heads, 8, T), F32),
            pltpu.VMEM((heads, 8, T), F32),
            pltpu.VMEM((KVH, T, GW * T), BF),
            pltpu.VMEM((KVH, 2 * T, HD), BF),
            pltpu.VMEM((KVH, 2 * T, HD), BF),
            pltpu.VMEM((KVH, HD, 2 * T), BF),
            pltpu.VMEM((KVH, T, HD), F32),
            pltpu.VMEM((KVH, T, HD), F32),
            pltpu.VMEM((4, HD // 2, T), F32),
            pltpu.VMEM((8, T), F32),
            pltpu.VMEM((8, T), F32),
            pltpu.VMEM((T, HD), F32),
            pltpu.VMEM((T, HD), F32),
            pltpu.VMEM((T, HD), F32),
            pltpu.VMEM((HD, T), F32),
            pltpu.VMEM((8, HD), F32),
            pltpu.VMEM((GW, T, T), F32),
            pltpu.VMEM((GW, T, T), F32),
            pltpu.VMEM((T, GW * T), BF),
            pltpu.VMEM((KVH, 2 * T, GW * T), BF),
            [pltpu.VMEM((NX, CH, 2, HD), BF)] * KVH,
            [pltpu.VMEM((2, CH, 2, HD), BF)] * KVH,
            pltpu.VMEM((KVH, T, 2, HD), BF),
            pltpu.VMEM((KVH, T, 2 * HD), BF),
            pltpu.VMEM((KVH, NX, CH, 2 * HD), BF),
            pltpu.VMEM((KVH, CH, 2 * HD), BF),
            pltpu.VMEM((KVH, CH, 2 * HD), BF),
            pltpu.VMEM((KVH, CH, 2 * HD), F32),
            pltpu.VMEM((KVH, T, 2 * HD), BF),
            pltpu.VMEM((8, 8, HD), F32),
            pltpu.VMEM((16, 8, HD), F32),
            pltpu.VMEM((16, 8, HD), F32),
            dma((2, KVH)),
            dma((7,)),
            dma((6,)),
            dma((KVH,)),
            dma((KVH,)),
            dma((KVH, NX)),
            dma((KVH, NX)),
            dma((KVH,)),
            dma((KVH,)),
            dma((KVH, NX)),
            dma((KVH, NX)),
            dma((KVH, NX)),
            dma((KVH, NX)),
            dma((KVH,)),
            dma((KVH,)),
            dma((KVH, NX)),
            dma((KVH, NX)),
            dma((8,)),
            dma((8,)),
            dma((16,)),
            dma((16,)),
            dma((16,)),
            dma((16,)),
        ],
        compiler_params=pltpu.CompilerParams(
            collective_id=0, has_side_effects=True, vmem_limit_bytes=56 << 20
        ),
    )(
        queries[0, 0], resp_kv[0, 0], prefix_kv[0, 0], norm_gains, dout[0, 0],
        lengths, rewards, owner, natural, transposed,
    )
    out = pl.pallas_call(
        finish,
        out_shape=shapes,
        in_specs=[anywhere] * 4,
        out_specs=[anywhere] * 4,
        scratch_shapes=[pltpu.VMEM(a.shape, a.dtype) for a in shapes] + [dma((7,)), dma((7,))],
        compiler_params=pltpu.CompilerParams(vmem_limit_bytes=56 << 20),
    )(*out)
    return (out[0][None, None], out[1][None, None], out[2][None, None], out[3])


def solution(mesh):
    return jax.shard_map(
        body,
        mesh=mesh,
        in_specs=(
            P("prompts", "group", None, None),
            P("prompts", "group", None, None, None),
            P("prompts", "group", None, None, None),
            P(),
            P("prompts", "group", None, None),
            P("prompts", "group"),
            P("prompts", "group"),
            P("prompts"),
        ),
        out_specs=(
            P("prompts", "group", None, None),
            P("prompts", "group", None, None, None),
            P("prompts", "group", None, None, None),
            P(),
        ),
        check_vma=False,
    )
```

```python
from functools import partial

import jax
import jax.numpy as jnp
import numpy as np
from jax import lax
from jax.experimental import pallas as pl
from jax.experimental.pallas import tpu as pltpu
from jax.sharding import PartitionSpec as P

HD = 128
T = 256
KVH = 4
GW = 8
NX = 4
CH = 64
EPSILON = 1e-06
THETA = 1000000.0
SCALE = HD**-0.5
LOG2E = 1.4426950408889634
LN2 = 0.6931471805599453
SHIFT = 40.0
F32 = jnp.float32
BF = jnp.bfloat16
MESH = pl.DeviceIdType.MESH


def nn(a, b):
    return lax.dot_general(a, b, (((1,), (0,)), ((), ())), preferred_element_type=F32)


def nt(a, b):
    return lax.dot_general(a, b, (((1,), (1,)), ((), ())), preferred_element_type=F32)


def tables():
    positions = T + np.arange(T, dtype=np.float64)
    angles = positions[:, None] * (THETA ** (-2.0 * np.arange(HD // 2) / HD))[None, :]
    c, s = np.cos(angles), np.sin(angles)
    natural = np.stack([np.concatenate([c, c], 1), np.concatenate([-s, s], 1)])
    return natural.astype(np.float32), np.stack([c.T, s.T]).astype(np.float32)


def kernel(
    q_hbm, kv_hbm, px_hbm, gain_hbm, do_hbm, len_hbm, rew_hbm, own_hbm, nat_hbm, tr_hbm,
    dq_hbm, dkv_hbm, dpx_hbm, dg_ref,
    gain_ref, nat_ref, tr_ref, len_ref, rew_ref, own_ref,
    q_vm, do_vm, kv_vm, px_vm, dkv_vm, dpx_vm,
    qn_s, qc_s, r_s, er_s, pr_s, se_s, sp_s, wr_s, kall, vall, kt_s, kn_s, rk_s, tabs, mask_s, adv_s,
    dkp, dkr, dva, gacc, gks,
    e_s, p_s, wb_s, gb_s,
    a_buf, b_buf, c_buf, r_buf, rr_buf, t_buf, tt_buf, tf_buf, ff_buf,
    rw_buf, ga_buf, gb_buf,
    in_sem, small_sem, out_sem, own_sem, px_sem,
    p1_s, p1_r, bz_s, bz_r, ag_s, ag_r, rs_s, rs_r, rz_s, rz_r, fg_s, fg_r,
    rw_s, rw_r, ga_s, ga_r, gb2_s, gb2_r,
):
    me = lax.axis_index("group")
    pr = lax.axis_index("prompts")
    my_x, my_z = lax.rem(me, NX), lax.div(me, NX)
    my_core, my_y, my_zl = lax.rem(pr, 2), lax.rem(lax.div(pr, 2), 4), lax.div(pr, 8)
    my_a = my_x * 4 + my_y
    my_b = (my_z * 4 + my_zl) * 2 + my_core
    z_peer = {"group": lax.rem(me + NX, 2 * NX), "prompts": pr}

    def x_peer(k):
        return {"group": my_z * NX + lax.rem(my_x + k, NX), "prompts": pr}

    def g_peer(k):
        return {"group": lax.rem(me + k, 2 * NX), "prompts": pr}

    def a_peer(k):
        a = lax.rem(my_a + k, 16)
        return {"group": my_z * 4 + lax.div(a, 4), "prompts": (my_zl * 4 + lax.rem(a, 4)) * 2 + my_core}

    def b_peer(k):
        b = lax.rem(my_b + k, 16)
        z = lax.div(b, 2)
        return {"group": lax.div(z, 4) * 4 + my_x, "prompts": (lax.rem(z, 4) * 4 + my_y) * 2 + lax.rem(b, 2)}

    def behind(mine, k, n):
        return lax.rem(mine + n - k, n)

    def remote(src, dst, ss, rs, dev):
        return pltpu.make_async_remote_copy(
            src_ref=src, dst_ref=dst, send_sem=ss, recv_sem=rs, device_id=dev, device_id_type=MESH
        )

    def greet(dev):
        pl.semaphore_signal(barrier, inc=1, device_id=dev, device_id_type=MESH)

    barrier = pltpu.get_barrier_semaphore()
    for k in range(15, 0, -1):
        greet(b_peer(k))
    for k in range(1, 16):
        greet(a_peer(k))
    for k in range(1, NX):
        greet({"group": (1 - my_z) * NX + lax.rem(my_x + k, NX), "prompts": pr})

    small = (
        (kv_hbm, kv_vm), (nat_hbm, nat_ref), (tr_hbm, tr_ref), (gain_hbm, gain_ref),
        (len_hbm, len_ref), (rew_hbm, rew_ref), (own_hbm, own_ref),
    )
    small_copies = [pltpu.make_async_copy(a, b, small_sem.at[i]) for i, (a, b) in enumerate(small)]

    def wide(g):
        return pl.ds(pl.multiple_of(g * (GW * HD), GW * HD), GW * HD)

    def in_copy(kind, g):
        src, dst = ((q_hbm, q_vm), (do_hbm, do_vm))[kind]
        return pltpu.make_async_copy(src.at[:, wide(g)], dst.at[:, wide(g)], in_sem.at[kind, g])

    def out_copy(g):
        return pltpu.make_async_copy(q_vm.at[:, wide(g)], dq_hbm.at[:, wide(g)], out_sem.at[g])

    def head_cols(g):
        return pl.ds(pl.multiple_of(g * HD, HD), HD)

    def rows(x):
        return pl.ds(pl.multiple_of(x * CH, CH), CH)

    def p1_copy(g, k, slot):
        src = px_vm.at[g, rows(lax.rem(my_x + k, NX))]
        return remote(src, a_buf[g].at[slot], p1_s.at[g, k], p1_r.at[g, k], x_peer(k))

    def own_copy(g):
        return pltpu.make_async_copy(px_vm.at[g, rows(my_x)], a_buf[g].at[my_x], own_sem.at[g])

    def px_copy(g):
        return pltpu.make_async_copy(px_hbm.at[:, :, head_cols(g)], px_vm.at[g], px_sem.at[KVH + g])

    for g in range(KVH):
        px_copy(g).start()
    for copy in small_copies:
        copy.start()
    for g in range(KVH):
        in_copy(0, g).start()
        in_copy(1, g).start()
    for copy in small_copies:
        copy.wait()

    rw_buf[me] = jnp.full((8, HD), rew_ref[0, 0].astype(F32), F32)
    gain_t = jnp.broadcast_to(gain_ref[0:1, :], (HD, HD)).T
    gain_t = jnp.concatenate([gain_t, gain_t], 1)
    cos_c, sin_c = tr_ref[0] * (SCALE * LOG2E), tr_ref[1] * (SCALE * LOG2E)
    tabs[0] = gain_t[:64] * cos_c
    tabs[1] = gain_t[64:] * sin_c
    tabs[2] = gain_t[64:] * cos_c
    tabs[3] = gain_t[:64] * sin_c
    gacc[...] = jnp.zeros_like(gacc)
    gks[...] = jnp.zeros_like(gks)
    gk = gain_ref[1:2, :]
    mask_s[...] = jnp.where(lax.broadcasted_iota(jnp.int32, (8, T), 1) < len_ref[0, 0], 1.0, 0.0)
    tri = lax.broadcasted_iota(jnp.int32, (HD, HD), 0) <= lax.broadcasted_iota(jnp.int32, (HD, HD), 1)
    owner = own_ref[0]
    owner_x, owner_z = lax.rem(owner, NX), lax.div(owner, NX)

    def rw_copy(k, slot):
        return remote(rw_buf.at[me], rw_buf.at[slot], rw_s.at[k], rw_r.at[k], g_peer(k))


    def bz_copy(g, slot):
        return remote(b_buf[g].at[my_z], b_buf[g].at[slot], bz_s.at[g], bz_r.at[g], z_peer)

    def ag_copy(g, k, x):
        return remote(c_buf.at[g, rows(my_x)], c_buf.at[g, rows(x)], ag_s.at[g, k], ag_r.at[g, k], x_peer(k))

    def bc1(g):
        own_copy(g).wait()
        for k in range(1, NX):
            p1_copy(g, k, behind(my_x, k, NX)).wait_recv()
        b_buf[g][my_z] = a_buf[g][owner_x]
        bz_copy(g, my_z).start()

    def bc2(g):
        bz_copy(g, 1 - my_z).wait_recv()
        c_buf[g, rows(my_x)] = b_buf[g][owner_z]
        for k in (2, 1, 3):
            ag_copy(g, k, my_x).start()

    def bc3(g):
        for k in range(1, NX):
            ag_copy(g, k, behind(my_x, k, NX)).wait_recv()
        kall[g, 0:T] = c_buf[g, :, 0, :]
        vall[g, 0:T] = c_buf[g, :, 1, :]
        kt_s[g] = kall[g].T

    def rs_copy(g, k, slot):
        src = r_buf.at[g, rows(lax.rem(my_x + k, NX))]
        return remote(src, rr_buf.at[g, slot], rs_s.at[g, k], rs_r.at[g, k], x_peer(k))

    def rz_copy(g):
        return remote(t_buf.at[g], tt_buf.at[g], rz_s.at[g], rz_r.at[g], z_peer)

    def fg_copy(g, k, x):
        return remote(ff_buf.at[g, rows(my_x)], ff_buf.at[g, rows(x)], fg_s.at[g, k], fg_r.at[g, k], x_peer(k))

    def rd1(g):
        adv = adv_s[0:1, 0:HD]
        r_buf[g, :, 0:HD] = (dkp[...] * (adv * LN2)).astype(BF)
        r_buf[g, :, HD:] = (dva[...] * adv).astype(BF)
        for k in (2, 1, 3):
            rs_copy(g, k, my_x).start()
        tf_buf[g, :, 0:HD] = dkp[rows(my_x)] * (adv * LN2)
        tf_buf[g, :, HD:] = dva[rows(my_x)] * adv

    def rd2(g):
        total = tf_buf[g]
        for k in range(1, NX):
            rs_copy(g, k, behind(my_x, k, NX)).wait_recv()
            total = total + rr_buf[g, behind(my_x, k, NX)].astype(F32)
        tf_buf[g] = total
        t_buf[g] = total.astype(BF)
        rz_copy(g).start()

    def rd3(g):
        rz_copy(g).wait_recv()
        ff_buf[g, rows(my_x)] = (tf_buf[g] + tt_buf[g].astype(F32)).astype(BF)
        for k in (2, 1, 3):
            fg_copy(g, k, my_x).start()

    def dpx_copy(g):
        cols = head_cols(g)
        return pltpu.make_async_copy(dpx_vm.at[:, :, cols], dpx_hbm.at[:, :, cols], px_sem.at[g])

    def rd4(g):
        for k in range(1, NX):
            fg_copy(g, k, behind(my_x, k, NX)).wait_recv()
        mine = owner == me
        cols = head_cols(g)
        dpx_vm[:, 0, cols] = jnp.where(mine, ff_buf[g, :, 0:HD], jnp.zeros((T, HD), BF))
        dpx_vm[:, 1, cols] = jnp.where(mine, ff_buf[g, :, HD:], jnp.zeros((T, HD), BF))
        dpx_copy(g).start()

    def key_prep(g, _):
        cols = head_cols(g)
        raw = kv_vm[:, 0, cols].astype(F32)
        rk = lax.rsqrt(jnp.mean(raw * raw, -1, keepdims=True) + EPSILON)
        kn = raw * rk
        kn_s[g] = kn
        rk_s[g] = jnp.broadcast_to(rk, (T, HD))
        kg = kn * gk
        kall[g, T : 2 * T] = (kg * nat_ref[0] + pltpu.roll(kg, HD // 2, 1) * nat_ref[1]).astype(BF)
        vall[g, T : 2 * T] = kv_vm[:, 1, cols]
        return 0

    lax.fori_loop(0, KVH, key_prep, 0)

    for g in range(KVH):
        px_copy(g).wait()
        own_copy(g).start()
    pl.semaphore_wait(barrier, 33)
    for g in range(KVH):
        for k in (2, 1, 3):
            p1_copy(g, k, my_x).start()
    for k in range(1, 8):
        rw_copy(k, me).start()

    def lanes(j):
        return slice(j * T, j * T + T)

    def cots(g):
        return jnp.concatenate([do_vm[:, head_cols(g * GW + j)] for j in range(GW)], 0)

    def first_part(g, j):
        h = g * GW + j
        cols = head_cols(h)
        cot = do_vm[:, cols]
        x = q_vm[:, cols].T.astype(F32)
        r = lax.rsqrt(jnp.sum(x * x, 0, keepdims=True) * (1.0 / HD) + EPSILON)
        qn = x * r
        qa, qb = qn[:64], qn[64:]
        r_s[h] = jnp.broadcast_to(r, (8, T))
        qn_s[h] = qn
        qc = jnp.concatenate([qa * tabs[0] - qb * tabs[1], qb * tabs[2] + qa * tabs[3]], 0).astype(BF)
        qc_s[g, :, lanes(j)] = qc
        sum_e = jnp.zeros((8, T), F32)
        sum_ep = jnp.zeros((8, T), F32)
        for s0 in range(0, T, HD):
            scores = nn(kall[g, T + s0 : T + s0 + HD], qc)
            prob = nt(vall[g, T + s0 : T + s0 + HD], cot)
            e = jnp.exp2(scores - SHIFT)
            if s0 == 0:
                e = jnp.concatenate([jnp.where(tri, e[:, :HD], 0.0), e[:, HD:]], 1)
            else:
                e = jnp.concatenate([jnp.zeros((HD, HD), F32), jnp.where(tri, e[:, HD:], 0.0)], 1)
            er_s[h, s0 : s0 + HD] = e
            pr_s[h, s0 : s0 + HD] = prob
            sum_e = sum_e + jnp.sum(e.reshape(HD // 8, 8, T), 0)
            sum_ep = sum_ep + jnp.sum((e * prob).reshape(HD // 8, 8, T), 0)
        se_s[h] = sum_e
        sp_s[h] = sum_ep

    def first_parts(g, _):
        in_copy(0, g).wait()
        in_copy(1, g).wait()
        for j in range(GW):
            first_part(g, j)

        @pl.when(g == 2)
        def _():
            bc1(0)
            bc1(1)

        @pl.when(g == 3)
        def _():
            bc1(2)
            bc1(3)

        return 0

    lax.fori_loop(0, KVH, first_parts, 0)

    for g in range(KVH):
        bc2(g)

    for k in range(1, 8):
        rw_copy(k, behind(me, k, 8)).wait_recv()
    total = rw_buf[0]
    square = rw_buf[0] * rw_buf[0]
    for k in range(1, 8):
        total = total + rw_buf[k]
        square = square + rw_buf[k] * rw_buf[k]
    mean = total / 8
    spread = jnp.sqrt(jnp.maximum(square / 8 - mean * mean, 0.0))
    advantage = (rw_buf[me] - mean) / jnp.maximum(spread, 1.0)
    adv_s[...] = jnp.concatenate([advantage, advantage], 1)

    def second_part(g, j):
        h = g * GW + j
        cols = head_cols(h)
        cot = do_vm[:, cols]
        qc = qc_s[g, :, lanes(j)]
        e_r, p_r = e_s.at[j], p_s.at[j]
        sum_e = se_s[h]
        sum_ep = sp_s[h]
        for s0 in range(0, T, HD):
            block = slice(s0, s0 + HD)
            scores = nn(kall[g, block], qc)
            prob = nt(vall[g, block], cot)
            e = jnp.exp2(scores - SHIFT)
            e_r[block] = e
            p_r[block] = prob
            sum_e = sum_e + jnp.sum(e.reshape(HD // 8, 8, T), 0)
            sum_ep = sum_ep + jnp.sum((e * prob).reshape(HD // 8, 8, T), 0)
        inv = mask_s[0:1] / jnp.sum(sum_e, 0, keepdims=True)
        dots = jnp.sum(sum_ep, 0, keepdims=True) * inv
        se_s[h] = jnp.broadcast_to(inv, (8, T))
        sp_s[h] = jnp.broadcast_to(dots, (8, T))
        for s0 in range(0, T, HD):
            block = slice(s0, s0 + HD)
            w = e_r[block] * inv
            wb_s[block, lanes(j)] = w.astype(BF)
            gb_s[g, block, lanes(j)] = (w * (p_r[block] - dots)).astype(BF)

    def second_parts(g, _):
        bc3(g)
        for j in range(GW):
            second_part(g, j)
        dva[...] = nn(wb_s[...], cots(g))
        dkp[...] = nt(gb_s[g, 0:T], qc_s[g])
        rd1(g)

        @pl.when(g == 3)
        def _():
            rd2(0)

        return 0

    lax.fori_loop(0, KVH, second_parts, 0)

    def third_part(g, j):
        h = g * GW + j
        cols = head_cols(h)
        inv = se_s[h, 0:1]
        dots = sp_s[h, 0:1]
        for s0 in range(0, T, HD):
            w = er_s[h, s0 : s0 + HD] * inv
            wr_s[g, s0 : s0 + HD, lanes(j)] = w.astype(BF)
            gb_s[g, T + s0 : T + s0 + HD, lanes(j)] = (w * (pr_s[h, s0 : s0 + HD] - dots)).astype(BF)
        dt = nn(kt_s[g], gb_s[g, :, lanes(j)])
        da, db = dt[:64], dt[64:]
        va = da * tabs[0] + db * tabs[3]
        vb = db * tabs[2] - da * tabs[1]
        er_s[h, 0:64] = va
        er_s[h, 64:HD] = vb
        return va * qn_s[h, 0:64], vb * qn_s[h, 64:HD]

    def query_grads(g, _):
        for j in range(GW):
            h = g * GW + j
            va, vb = er_s[h, 0:64], er_s[h, 64:HD]
            qa, qb = qn_s[h, 0:64], qn_s[h, 64:HD]
            m = jnp.sum(va * qa + vb * qb, 0, keepdims=True) * (1.0 / HD)
            r = r_s[h, 0:1] * (adv_s[0:1] * LN2)
            dx = jnp.concatenate([(va - qa * m) * r, (vb - qb * m) * r], 0).astype(BF)
            q_vm[:, head_cols(h)] = dx.T
        out_copy(g).start()
        return 0

    def key_grads(g):
        dk = dkr[...] * LN2
        u = dk * nat_ref[0] - pltpu.roll(dk, HD // 2, 1) * nat_ref[1]
        kn = kn_s[g]
        gks[0:1] += jnp.sum(u * kn, 0, keepdims=True)
        v = u * gk
        m = jnp.mean(v * kn, -1, keepdims=True)
        dkv_vm[:, 0, head_cols(g)] = (rk_s[g] * adv_s[0:1, 0:HD] * (v - kn * m)).astype(BF)

    def third_parts(g, _):
        sum_a = sum_b = jnp.zeros((HD // 2, T), F32)
        for j in range(GW):
            pa, pb = third_part(g, j)
            sum_a, sum_b = sum_a + pa, sum_b + pb
        gacc[0:64] += sum_a
        gacc[64:HD] += sum_b
        dkr[...] = nt(gb_s[g, T : 2 * T], qc_s[g])
        key_grads(g)

        @pl.when(g == 0)
        def _():
            rd2(1)

        @pl.when(g == 1)
        def _():
            rd2(2)

        @pl.when(g == 2)
        def _():
            rd2(3)

        return 0

    lax.fori_loop(0, KVH, third_parts, 0)
    last = KVH - 1

    def stage(buf, mine, peer, ss, rs, order):
        def copy(k, slot):
            return remote(buf.at[mine], buf.at[slot], ss.at[k], rs.at[k], peer(k))

        def start():
            for k in order:
                copy(k, mine).start()

        def finish():
            for k in range(1, 16):
                copy(k, behind(mine, k, 16)).wait_recv()
            out = buf[0]
            for k in range(1, 16):
                out = out + buf[k]
            return out

        def drain():
            for k in range(1, 16):
                copy(k, mine).wait_send()

        return start, finish, drain

    ga_start, ga_finish, ga_drain = stage(
        ga_buf, my_a, a_peer, ga_s, ga_r, (10, 6, 9, 11, 7, 5, 14, 13, 2, 8, 3, 15, 1, 12, 4)
    )
    gb_start, gb_finish, gb_drain = stage(
        gb_buf, my_b, b_peer, gb2_s, gb2_r, (8, 9, 7, 10, 6, 11, 5, 12, 4, 13, 3, 14, 2, 15, 1)
    )

    gq = jnp.broadcast_to(jnp.sum(gacc[...], 1, keepdims=True), (HD, HD)).T * LN2 / gain_ref[0:1, :]
    ga_buf[my_a] = jnp.concatenate([gq[0:1], gks[0:1], jnp.zeros((6, HD), F32)], 0) * adv_s[:, 0:HD]
    ga_start()
    rd3(0)
    lax.fori_loop(0, KVH, query_grads, 0)

    def value_grads(g, _):
        total = nn(wr_s[g], cots(g))
        dkv_vm[:, 1, head_cols(g)] = (total * adv_s[0:1, 0:HD]).astype(BF)
        return 0

    rd3(1)
    rd3(2)
    lax.fori_loop(0, KVH, value_grads, 0)
    dkv_copy = pltpu.make_async_copy(dkv_vm, dkv_hbm, out_sem.at[4])
    dkv_copy.start()
    rd3(last)
    gb_buf[my_b] = ga_finish()
    gb_start()
    rd4(0)
    rd4(1)
    rd4(2)
    for k in range(1, 8):
        rw_copy(k, me).wait_send()
    ga_drain()
    for g in range(KVH):
        bz_copy(g, my_z).wait_send()
        rz_copy(g).wait_send()
        for k in range(1, NX):
            p1_copy(g, k, my_x).wait_send()
            ag_copy(g, k, my_x).wait_send()
            rs_copy(g, k, my_x).wait_send()
        out_copy(g).wait()
    dkv_copy.wait()
    rd4(last)
    dg_ref[...] = gb_finish()[0:2] * (1.0 / 256)
    gb_drain()
    for g in range(KVH):
        for k in range(1, NX):
            fg_copy(g, k, my_x).wait_send()
        dpx_copy(g).wait()


def finish(*refs):
    sources, results, held, in_sem, out_sem = refs[:4], refs[4:8], refs[8:12], refs[12], refs[13]
    parts = [(0, pl.ds(i * 64, 64)) for i in range(4)] + [(1, pl.ds(0, T)), (2, pl.ds(0, T)), (3, pl.ds(0, 2))]
    arrive = [pltpu.make_async_copy(sources[a].at[p], held[a].at[p], in_sem.at[i]) for i, (a, p) in enumerate(parts)]
    leave = [pltpu.make_async_copy(held[a].at[p], results[a].at[p], out_sem.at[i]) for i, (a, p) in enumerate(parts)]
    for copy in arrive:
        copy.start()
    for came, goes in zip(arrive, leave):
        came.wait()
        goes.start()
    for copy in leave:
        copy.wait()


def body(queries, resp_kv, prefix_kv, norm_gains, dout, lengths, rewards, owner):
    natural, transposed = tables()
    anywhere = pl.BlockSpec(memory_space=pl.ANY)
    vmem = pl.BlockSpec(memory_space=pltpu.VMEM)
    dma = pltpu.SemaphoreType.DMA
    heads = KVH * GW
    shapes = [
        jax.ShapeDtypeStruct((T, 4096), BF),
        jax.ShapeDtypeStruct((T, 2, 512), BF),
        jax.ShapeDtypeStruct((T, 2, 512), BF),
        jax.ShapeDtypeStruct((2, HD), F32),
    ]
    out = pl.pallas_call(
        kernel,
        out_shape=shapes,
        in_specs=[anywhere] * 10,
        out_specs=[anywhere, anywhere, anywhere, vmem],
        scratch_shapes=[
            pltpu.VMEM((2, HD), F32),
            pltpu.VMEM((2, T, HD), F32),
            pltpu.VMEM((2, HD // 2, T), F32),
            pltpu.SMEM((1, 1), jnp.int32),
            pltpu.SMEM((1, 1), jnp.int32),
            pltpu.SMEM((1,), jnp.int32),
            pltpu.VMEM((T, 4096), BF),
            pltpu.VMEM((T, 4096), BF),
            pltpu.VMEM((T, 2, 512), BF),
            pltpu.VMEM((KVH, T, 2, HD), BF),
            pltpu.VMEM((T, 2, 512), BF),
            pltpu.VMEM((T, 2, 512), BF),
            pltpu.VMEM((heads, HD, T), F32),
            pltpu.VMEM((KVH, HD, GW * T), BF),
            pltpu.VMEM((heads, 8, T), F32),
            pltpu.VMEM((heads, T, T), F32),
            pltpu.VMEM((heads, T, T), F32),
            pltpu.VMEM((heads, 8, T), F32),
            pltpu.VMEM((heads, 8, T), F32),
            pltpu.VMEM((KVH, T, GW * T), BF),
            pltpu.VMEM((KVH, 2 * T, HD), BF),
            pltpu.VMEM((KVH, 2 * T, HD), BF),
            pltpu.VMEM((KVH, HD, 2 * T), BF),
            pltpu.VMEM((KVH, T, HD), F32),
            pltpu.VMEM((KVH, T, HD), F32),
            pltpu.VMEM((4, HD // 2, T), F32),
            pltpu.VMEM((8, T), F32),
            pltpu.VMEM((8, T), F32),
            pltpu.VMEM((T, HD), F32),
            pltpu.VMEM((T, HD), F32),
            pltpu.VMEM((T, HD), F32),
            pltpu.VMEM((HD, T), F32),
            pltpu.VMEM((8, HD), F32),
            pltpu.VMEM((GW, T, T), F32),
            pltpu.VMEM((GW, T, T), F32),
            pltpu.VMEM((T, GW * T), BF),
            pltpu.VMEM((KVH, 2 * T, GW * T), BF),
            [pltpu.VMEM((NX, CH, 2, HD), BF)] * KVH,
            [pltpu.VMEM((2, CH, 2, HD), BF)] * KVH,
            pltpu.VMEM((KVH, T, 2, HD), BF),
            pltpu.VMEM((KVH, T, 2 * HD), BF),
            pltpu.VMEM((KVH, NX, CH, 2 * HD), BF),
            pltpu.VMEM((KVH, CH, 2 * HD), BF),
            pltpu.VMEM((KVH, CH, 2 * HD), BF),
            pltpu.VMEM((KVH, CH, 2 * HD), F32),
            pltpu.VMEM((KVH, T, 2 * HD), BF),
            pltpu.VMEM((8, 8, HD), F32),
            pltpu.VMEM((16, 8, HD), F32),
            pltpu.VMEM((16, 8, HD), F32),
            dma((2, KVH)),
            dma((7,)),
            dma((6,)),
            dma((KVH,)),
            dma((2 * KVH,)),
            dma((KVH, NX)),
            dma((KVH, NX)),
            dma((KVH,)),
            dma((KVH,)),
            dma((KVH, NX)),
            dma((KVH, NX)),
            dma((KVH, NX)),
            dma((KVH, NX)),
            dma((KVH,)),
            dma((KVH,)),
            dma((KVH, NX)),
            dma((KVH, NX)),
            dma((8,)),
            dma((8,)),
            dma((16,)),
            dma((16,)),
            dma((16,)),
            dma((16,)),
        ],
        compiler_params=pltpu.CompilerParams(
            collective_id=0, has_side_effects=True, vmem_limit_bytes=56 << 20
        ),
    )(
        queries[0, 0], resp_kv[0, 0], prefix_kv[0, 0], norm_gains, dout[0, 0],
        lengths, rewards, owner, natural, transposed,
    )
    out = pl.pallas_call(
        finish,
        out_shape=shapes,
        in_specs=[anywhere] * 4,
        out_specs=[anywhere] * 4,
        scratch_shapes=[pltpu.VMEM(a.shape, a.dtype) for a in shapes] + [dma((7,)), dma((7,))],
        compiler_params=pltpu.CompilerParams(vmem_limit_bytes=56 << 20),
    )(*out)
    return (out[0][None, None], out[1][None, None], out[2][None, None], out[3])


def solution(mesh):
    return jax.shard_map(
        body,
        mesh=mesh,
        in_specs=(
            P("prompts", "group", None, None),
            P("prompts", "group", None, None, None),
            P("prompts", "group", None, None, None),
            P(),
            P("prompts", "group", None, None),
            P("prompts", "group"),
            P("prompts", "group"),
            P("prompts"),
        ),
        out_specs=(
            P("prompts", "group", None, None),
            P("prompts", "group", None, None, None),
            P("prompts", "group", None, None, None),
            P(),
        ),
        check_vma=False,
    )
```

```python
from functools import partial

import jax
import jax.numpy as jnp
import numpy as np
from jax import lax
from jax.experimental import pallas as pl
from jax.experimental.pallas import tpu as pltpu
from jax.sharding import PartitionSpec as P

HD = 128
T = 256
KVH = 4
GW = 8
NX = 4
CH = 64
EPSILON = 1e-06
THETA = 1000000.0
SCALE = HD**-0.5
LOG2E = 1.4426950408889634
LN2 = 0.6931471805599453
SHIFT = 40.0
F32 = jnp.float32
BF = jnp.bfloat16
MESH = pl.DeviceIdType.MESH


def nn(a, b):
    return lax.dot_general(a, b, (((1,), (0,)), ((), ())), preferred_element_type=F32)


def nt(a, b):
    return lax.dot_general(a, b, (((1,), (1,)), ((), ())), preferred_element_type=F32)


def tables():
    positions = T + np.arange(T, dtype=np.float64)
    angles = positions[:, None] * (THETA ** (-2.0 * np.arange(HD // 2) / HD))[None, :]
    c, s = np.cos(angles), np.sin(angles)
    natural = np.stack([np.concatenate([c, c], 1), np.concatenate([-s, s], 1)])
    return natural.astype(np.float32), np.stack([c.T, s.T]).astype(np.float32)


def kernel(
    q_hbm, kv_hbm, px_hbm, gain_hbm, do_hbm, len_hbm, rew_hbm, own_hbm, nat_hbm, tr_hbm,
    dq_hbm, dkv_hbm, dpx_hbm, dg_ref,
    gain_ref, nat_ref, tr_ref, len_ref, rew_ref, own_ref,
    q_vm, do_vm, kv_vm, px_vm, dkv_vm, dpx_vm,
    qn_s, qc_s, r_s, er_s, pr_s, se_s, sp_s, wr_s, kall, vall, kt_s, kn_s, rk_s, tabs, mask_s, adv_s,
    dkp, dkr, dva, gacc, gks,
    e_s, p_s, wb_s, gb_s,
    a_buf, b_buf, c_buf, r_buf, rr_buf, t_buf, tt_buf, tf_buf, ff_buf,
    rw_buf, ga_buf, gb_buf,
    in_sem, small_sem, out_sem, own_sem, px_sem,
    p1_s, p1_r, bz_s, bz_r, ag_s, ag_r, rs_s, rs_r, rz_s, rz_r, fg_s, fg_r,
    rw_s, rw_r, ga_s, ga_r, gb2_s, gb2_r,
):
    me = lax.axis_index("group")
    pr = lax.axis_index("prompts")
    my_x, my_z = lax.rem(me, NX), lax.div(me, NX)
    my_core, my_y, my_zl = lax.rem(pr, 2), lax.rem(lax.div(pr, 2), 4), lax.div(pr, 8)
    my_a = my_x * 4 + my_y
    my_b = (my_z * 4 + my_zl) * 2 + my_core
    z_peer = {"group": lax.rem(me + NX, 2 * NX), "prompts": pr}

    def x_peer(k):
        return {"group": my_z * NX + lax.rem(my_x + k, NX), "prompts": pr}

    def g_peer(k):
        return {"group": lax.rem(me + k, 2 * NX), "prompts": pr}

    def a_peer(k):
        a = lax.rem(my_a + k, 16)
        return {"group": my_z * 4 + lax.div(a, 4), "prompts": (my_zl * 4 + lax.rem(a, 4)) * 2 + my_core}

    def b_peer(k):
        b = lax.rem(my_b + k, 16)
        z = lax.div(b, 2)
        return {"group": lax.div(z, 4) * 4 + my_x, "prompts": (lax.rem(z, 4) * 4 + my_y) * 2 + lax.rem(b, 2)}

    def behind(mine, k, n):
        return lax.rem(mine + n - k, n)

    def remote(src, dst, ss, rs, dev):
        return pltpu.make_async_remote_copy(
            src_ref=src, dst_ref=dst, send_sem=ss, recv_sem=rs, device_id=dev, device_id_type=MESH
        )

    def greet(dev):
        pl.semaphore_signal(barrier, inc=1, device_id=dev, device_id_type=MESH)

    barrier = pltpu.get_barrier_semaphore()
    for k in range(15, 0, -1):
        greet(b_peer(k))
    for k in range(1, 16):
        greet(a_peer(k))
    for k in range(1, NX):
        greet({"group": (1 - my_z) * NX + lax.rem(my_x + k, NX), "prompts": pr})

    small = (
        (kv_hbm, kv_vm), (nat_hbm, nat_ref), (tr_hbm, tr_ref), (gain_hbm, gain_ref),
        (len_hbm, len_ref), (rew_hbm, rew_ref), (own_hbm, own_ref),
    )
    small_copies = [pltpu.make_async_copy(a, b, small_sem.at[i]) for i, (a, b) in enumerate(small)]

    def wide(g):
        return pl.ds(pl.multiple_of(g * (GW * HD), GW * HD), GW * HD)

    def in_copy(kind, g):
        src, dst = ((q_hbm, q_vm), (do_hbm, do_vm))[kind]
        return pltpu.make_async_copy(src.at[:, wide(g)], dst.at[:, wide(g)], in_sem.at[kind, g])

    def out_copy(g):
        return pltpu.make_async_copy(q_vm.at[:, wide(g)], dq_hbm.at[:, wide(g)], out_sem.at[g])

    def head_cols(g):
        return pl.ds(pl.multiple_of(g * HD, HD), HD)

    def rows(x):
        return pl.ds(pl.multiple_of(x * CH, CH), CH)

    def p1_copy(g, k, slot):
        src = px_vm.at[g, rows(lax.rem(my_x + k, NX))]
        return remote(src, a_buf[g].at[slot], p1_s.at[g, k], p1_r.at[g, k], x_peer(k))

    def own_copy(g):
        return pltpu.make_async_copy(px_vm.at[g, rows(my_x)], a_buf[g].at[my_x], own_sem.at[g])

    def px_copy(g):
        return pltpu.make_async_copy(px_hbm.at[:, :, head_cols(g)], px_vm.at[g], px_sem.at[KVH + g])

    for g in range(KVH):
        px_copy(g).start()
    for copy in small_copies:
        copy.start()
    for g in range(KVH):
        in_copy(0, g).start()
        in_copy(1, g).start()
    for copy in small_copies:
        copy.wait()

    rw_buf[me] = jnp.full((8, HD), rew_ref[0, 0].astype(F32), F32)
    gain_t = jnp.broadcast_to(gain_ref[0:1, :], (HD, HD)).T
    gain_t = jnp.concatenate([gain_t, gain_t], 1)
    cos_c, sin_c = tr_ref[0] * (SCALE * LOG2E), tr_ref[1] * (SCALE * LOG2E)
    tabs[0] = gain_t[:64] * cos_c
    tabs[1] = gain_t[64:] * sin_c
    tabs[2] = gain_t[64:] * cos_c
    tabs[3] = gain_t[:64] * sin_c
    gacc[...] = jnp.zeros_like(gacc)
    gks[...] = jnp.zeros_like(gks)
    gk = gain_ref[1:2, :]
    mask_s[...] = jnp.where(lax.broadcasted_iota(jnp.int32, (8, T), 1) < len_ref[0, 0], 1.0, 0.0)
    tri = lax.broadcasted_iota(jnp.int32, (HD, HD), 0) <= lax.broadcasted_iota(jnp.int32, (HD, HD), 1)
    owner = own_ref[0]
    owner_x, owner_z = lax.rem(owner, NX), lax.div(owner, NX)

    def rw_copy(k, slot):
        return remote(rw_buf.at[me], rw_buf.at[slot], rw_s.at[k], rw_r.at[k], g_peer(k))


    def bz_copy(g, slot):
        return remote(b_buf[g].at[my_z], b_buf[g].at[slot], bz_s.at[g], bz_r.at[g], z_peer)

    def ag_copy(g, k, x):
        return remote(c_buf.at[g, rows(my_x)], c_buf.at[g, rows(x)], ag_s.at[g, k], ag_r.at[g, k], x_peer(k))

    def bc1(g):
        own_copy(g).wait()
        for k in range(1, NX):
            p1_copy(g, k, behind(my_x, k, NX)).wait_recv()
        b_buf[g][my_z] = a_buf[g][owner_x]
        bz_copy(g, my_z).start()

    def bc2(g):
        bz_copy(g, 1 - my_z).wait_recv()
        c_buf[g, rows(my_x)] = b_buf[g][owner_z]
        for k in (2, 1, 3):
            ag_copy(g, k, my_x).start()

    def bc3(g):
        for k in range(1, NX):
            ag_copy(g, k, behind(my_x, k, NX)).wait_recv()
        kall[g, 0:T] = c_buf[g, :, 0, :]
        vall[g, 0:T] = c_buf[g, :, 1, :]
        kt_s[g] = kall[g].T

    def rs_copy(g, k, slot):
        src = r_buf.at[g, rows(lax.rem(my_x + k, NX))]
        return remote(src, rr_buf.at[g, slot], rs_s.at[g, k], rs_r.at[g, k], x_peer(k))

    def rz_copy(g):
        return remote(t_buf.at[g], tt_buf.at[g], rz_s.at[g], rz_r.at[g], z_peer)

    def fg_copy(g, k, x):
        return remote(ff_buf.at[g, rows(my_x)], ff_buf.at[g, rows(x)], fg_s.at[g, k], fg_r.at[g, k], x_peer(k))

    def rd1(g):
        adv = adv_s[0:1, 0:HD]
        r_buf[g, :, 0:HD] = (dkp[...] * (adv * LN2)).astype(BF)
        r_buf[g, :, HD:] = (dva[...] * adv).astype(BF)
        for k in (2, 1, 3):
            rs_copy(g, k, my_x).start()
        tf_buf[g, :, 0:HD] = dkp[rows(my_x)] * (adv * LN2)
        tf_buf[g, :, HD:] = dva[rows(my_x)] * adv

    def rd2(g):
        total = tf_buf[g]
        for k in range(1, NX):
            rs_copy(g, k, behind(my_x, k, NX)).wait_recv()
            total = total + rr_buf[g, behind(my_x, k, NX)].astype(F32)
        tf_buf[g] = total
        t_buf[g] = total.astype(BF)
        rz_copy(g).start()

    def rd3(g):
        rz_copy(g).wait_recv()
        ff_buf[g, rows(my_x)] = (tf_buf[g] + tt_buf[g].astype(F32)).astype(BF)
        for k in (2, 1, 3):
            fg_copy(g, k, my_x).start()

    def dpx_copy(g):
        cols = head_cols(g)
        return pltpu.make_async_copy(dpx_vm.at[:, :, cols], dpx_hbm.at[:, :, cols], px_sem.at[g])

    def rd4(g):
        for k in range(1, NX):
            fg_copy(g, k, behind(my_x, k, NX)).wait_recv()
        mine = owner == me
        cols = head_cols(g)
        dpx_vm[:, 0, cols] = jnp.where(mine, ff_buf[g, :, 0:HD], jnp.zeros((T, HD), BF))
        dpx_vm[:, 1, cols] = jnp.where(mine, ff_buf[g, :, HD:], jnp.zeros((T, HD), BF))
        dpx_copy(g).start()

    def key_prep(g, _):
        cols = head_cols(g)
        raw = kv_vm[:, 0, cols].astype(F32)
        rk = lax.rsqrt(jnp.mean(raw * raw, -1, keepdims=True) + EPSILON)
        kn = raw * rk
        kn_s[g] = kn
        rk_s[g] = jnp.broadcast_to(rk, (T, HD))
        kg = kn * gk
        kall[g, T : 2 * T] = (kg * nat_ref[0] + pltpu.roll(kg, HD // 2, 1) * nat_ref[1]).astype(BF)
        vall[g, T : 2 * T] = kv_vm[:, 1, cols]
        return 0

    lax.fori_loop(0, KVH, key_prep, 0)

    for g in range(KVH):
        px_copy(g).wait()
        own_copy(g).start()
    pl.semaphore_wait(barrier, 33)
    for g in range(KVH):
        for k in (2, 1, 3):
            p1_copy(g, k, my_x).start()
    for k in range(1, 8):
        rw_copy(k, me).start()

    def lanes(j):
        return slice(j * T, j * T + T)

    def cots(g):
        return jnp.concatenate([do_vm[:, head_cols(g * GW + j)] for j in range(GW)], 0)

    def first_part(g, j):
        h = g * GW + j
        cols = head_cols(h)
        cot = do_vm[:, cols]
        x = q_vm[:, cols].T.astype(F32)
        r = lax.rsqrt(jnp.sum(x * x, 0, keepdims=True) * (1.0 / HD) + EPSILON)
        qn = x * r
        qa, qb = qn[:64], qn[64:]
        r_s[h] = jnp.broadcast_to(r, (8, T))
        qn_s[h] = qn
        qc = jnp.concatenate([qa * tabs[0] - qb * tabs[1], qb * tabs[2] + qa * tabs[3]], 0).astype(BF)
        qc_s[g, :, lanes(j)] = qc
        sum_e = jnp.zeros((8, T), F32)
        sum_ep = jnp.zeros((8, T), F32)
        for s0 in range(0, T, HD):
            scores = nn(kall[g, T + s0 : T + s0 + HD], qc)
            prob = nt(vall[g, T + s0 : T + s0 + HD], cot)
            e = jnp.exp2(scores - SHIFT)
            if s0 == 0:
                e = jnp.concatenate([jnp.where(tri, e[:, :HD], 0.0), e[:, HD:]], 1)
            else:
                e = jnp.concatenate([jnp.zeros((HD, HD), F32), jnp.where(tri, e[:, HD:], 0.0)], 1)
            er_s[h, s0 : s0 + HD] = e
            pr_s[h, s0 : s0 + HD] = prob
            sum_e = sum_e + jnp.sum(e.reshape(HD // 8, 8, T), 0)
            sum_ep = sum_ep + jnp.sum((e * prob).reshape(HD // 8, 8, T), 0)
        se_s[h] = sum_e
        sp_s[h] = sum_ep

    def first_parts(g, _):
        in_copy(0, g).wait()
        in_copy(1, g).wait()
        for j in range(GW):
            first_part(g, j)

        @pl.when(g == 1)
        def _():
            bc1(0)

        @pl.when(g == 2)
        def _():
            bc1(1)

        @pl.when(g == 3)
        def _():
            bc1(2)
            bc1(3)

        return 0

    lax.fori_loop(0, KVH, first_parts, 0)

    for g in range(KVH):
        bc2(g)

    for k in range(1, 8):
        rw_copy(k, behind(me, k, 8)).wait_recv()
    total = rw_buf[0]
    square = rw_buf[0] * rw_buf[0]
    for k in range(1, 8):
        total = total + rw_buf[k]
        square = square + rw_buf[k] * rw_buf[k]
    mean = total / 8
    spread = jnp.sqrt(jnp.maximum(square / 8 - mean * mean, 0.0))
    advantage = (rw_buf[me] - mean) / jnp.maximum(spread, 1.0)
    adv_s[...] = jnp.concatenate([advantage, advantage], 1)

    def second_part(g, j):
        h = g * GW + j
        cols = head_cols(h)
        cot = do_vm[:, cols]
        qc = qc_s[g, :, lanes(j)]
        e_r, p_r = e_s.at[j], p_s.at[j]
        sum_e = se_s[h]
        sum_ep = sp_s[h]
        for s0 in range(0, T, HD):
            block = slice(s0, s0 + HD)
            scores = nn(kall[g, block], qc)
            prob = nt(vall[g, block], cot)
            e = jnp.exp2(scores - SHIFT)
            e_r[block] = e
            p_r[block] = prob
            sum_e = sum_e + jnp.sum(e.reshape(HD // 8, 8, T), 0)
            sum_ep = sum_ep + jnp.sum((e * prob).reshape(HD // 8, 8, T), 0)
        inv = mask_s[0:1] / jnp.sum(sum_e, 0, keepdims=True)
        dots = jnp.sum(sum_ep, 0, keepdims=True) * inv
        se_s[h] = jnp.broadcast_to(inv, (8, T))
        sp_s[h] = jnp.broadcast_to(dots, (8, T))
        for s0 in range(0, T, HD):
            block = slice(s0, s0 + HD)
            w = e_r[block] * inv
            wb_s[block, lanes(j)] = w.astype(BF)
            gb_s[g, block, lanes(j)] = (w * (p_r[block] - dots)).astype(BF)

    def second_parts(g, _):
        bc3(g)
        for j in range(GW):
            second_part(g, j)
        dva[...] = nn(wb_s[...], cots(g))
        dkp[...] = nt(gb_s[g, 0:T], qc_s[g])
        rd1(g)

        @pl.when(g == 3)
        def _():
            rd2(0)

        return 0

    lax.fori_loop(0, KVH, second_parts, 0)

    def third_part(g, j):
        h = g * GW + j
        cols = head_cols(h)
        inv = se_s[h, 0:1]
        dots = sp_s[h, 0:1]
        for s0 in range(0, T, HD):
            w = er_s[h, s0 : s0 + HD] * inv
            wr_s[g, s0 : s0 + HD, lanes(j)] = w.astype(BF)
            gb_s[g, T + s0 : T + s0 + HD, lanes(j)] = (w * (pr_s[h, s0 : s0 + HD] - dots)).astype(BF)
        dt = nn(kt_s[g], gb_s[g, :, lanes(j)])
        da, db = dt[:64], dt[64:]
        va = da * tabs[0] + db * tabs[3]
        vb = db * tabs[2] - da * tabs[1]
        er_s[h, 0:64] = va
        er_s[h, 64:HD] = vb
        return va * qn_s[h, 0:64], vb * qn_s[h, 64:HD]

    def query_grads(g, _):
        for j in range(GW):
            h = g * GW + j
            va, vb = er_s[h, 0:64], er_s[h, 64:HD]
            qa, qb = qn_s[h, 0:64], qn_s[h, 64:HD]
            m = jnp.sum(va * qa + vb * qb, 0, keepdims=True) * (1.0 / HD)
            r = r_s[h, 0:1] * (adv_s[0:1] * LN2)
            dx = jnp.concatenate([(va - qa * m) * r, (vb - qb * m) * r], 0).astype(BF)
            q_vm[:, head_cols(h)] = dx.T
        out_copy(g).start()
        return 0

    def key_grads(g):
        dk = dkr[...] * LN2
        u = dk * nat_ref[0] - pltpu.roll(dk, HD // 2, 1) * nat_ref[1]
        kn = kn_s[g]
        gks[0:1] += jnp.sum(u * kn, 0, keepdims=True)
        v = u * gk
        m = jnp.mean(v * kn, -1, keepdims=True)
        dkv_vm[:, 0, head_cols(g)] = (rk_s[g] * adv_s[0:1, 0:HD] * (v - kn * m)).astype(BF)

    def third_parts(g, _):
        sum_a = sum_b = jnp.zeros((HD // 2, T), F32)
        for j in range(GW):
            pa, pb = third_part(g, j)
            sum_a, sum_b = sum_a + pa, sum_b + pb
        gacc[0:64] += sum_a
        gacc[64:HD] += sum_b
        dkr[...] = nt(gb_s[g, T : 2 * T], qc_s[g])
        key_grads(g)

        @pl.when(g == 0)
        def _():
            rd2(1)

        @pl.when(g == 1)
        def _():
            rd2(2)

        @pl.when(g == 2)
        def _():
            rd2(3)

        return 0

    lax.fori_loop(0, KVH, third_parts, 0)
    last = KVH - 1

    def stage(buf, mine, peer, ss, rs, order):
        def copy(k, slot):
            return remote(buf.at[mine], buf.at[slot], ss.at[k], rs.at[k], peer(k))

        def start():
            for k in order:
                copy(k, mine).start()

        def finish():
            for k in range(1, 16):
                copy(k, behind(mine, k, 16)).wait_recv()
            out = buf[0]
            for k in range(1, 16):
                out = out + buf[k]
            return out

        def drain():
            for k in range(1, 16):
                copy(k, mine).wait_send()

        return start, finish, drain

    ga_start, ga_finish, ga_drain = stage(
        ga_buf, my_a, a_peer, ga_s, ga_r, (10, 6, 9, 11, 7, 5, 14, 13, 2, 8, 3, 15, 1, 12, 4)
    )
    gb_start, gb_finish, gb_drain = stage(
        gb_buf, my_b, b_peer, gb2_s, gb2_r, (8, 9, 7, 10, 6, 11, 5, 12, 4, 13, 3, 14, 2, 15, 1)
    )

    gq = jnp.broadcast_to(jnp.sum(gacc[...], 1, keepdims=True), (HD, HD)).T * LN2 / gain_ref[0:1, :]
    ga_buf[my_a] = jnp.concatenate([gq[0:1], gks[0:1], jnp.zeros((6, HD), F32)], 0) * adv_s[:, 0:HD]
    ga_start()
    rd3(0)
    lax.fori_loop(0, KVH, query_grads, 0)

    def value_grads(g, _):
        total = nn(wr_s[g], cots(g))
        dkv_vm[:, 1, head_cols(g)] = (total * adv_s[0:1, 0:HD]).astype(BF)
        return 0

    rd3(1)
    rd3(2)
    rd3(last)
    gb_buf[my_b] = ga_finish()
    gb_start()
    lax.fori_loop(0, KVH, value_grads, 0)
    dkv_copy = pltpu.make_async_copy(dkv_vm, dkv_hbm, out_sem.at[4])
    dkv_copy.start()
    rd4(0)
    rd4(1)
    rd4(2)
    for k in range(1, 8):
        rw_copy(k, me).wait_send()
    ga_drain()
    for g in range(KVH):
        bz_copy(g, my_z).wait_send()
        rz_copy(g).wait_send()
        for k in range(1, NX):
            p1_copy(g, k, my_x).wait_send()
            ag_copy(g, k, my_x).wait_send()
            rs_copy(g, k, my_x).wait_send()
        out_copy(g).wait()
    dkv_copy.wait()
    rd4(last)
    dg_ref[...] = gb_finish()[0:2] * (1.0 / 256)
    gb_drain()
    for g in range(KVH):
        for k in range(1, NX):
            fg_copy(g, k, my_x).wait_send()
        dpx_copy(g).wait()


def finish(*refs):
    sources, results, held, in_sem, out_sem = refs[:4], refs[4:8], refs[8:12], refs[12], refs[13]
    parts = [(0, pl.ds(i * 64, 64)) for i in range(4)] + [(1, pl.ds(0, T)), (2, pl.ds(0, T)), (3, pl.ds(0, 2))]
    arrive = [pltpu.make_async_copy(sources[a].at[p], held[a].at[p], in_sem.at[i]) for i, (a, p) in enumerate(parts)]
    leave = [pltpu.make_async_copy(held[a].at[p], results[a].at[p], out_sem.at[i]) for i, (a, p) in enumerate(parts)]
    for copy in arrive:
        copy.start()
    for came, goes in zip(arrive, leave):
        came.wait()
        goes.start()
    for copy in leave:
        copy.wait()


def body(queries, resp_kv, prefix_kv, norm_gains, dout, lengths, rewards, owner):
    natural, transposed = tables()
    anywhere = pl.BlockSpec(memory_space=pl.ANY)
    vmem = pl.BlockSpec(memory_space=pltpu.VMEM)
    dma = pltpu.SemaphoreType.DMA
    heads = KVH * GW
    shapes = [
        jax.ShapeDtypeStruct((T, 4096), BF),
        jax.ShapeDtypeStruct((T, 2, 512), BF),
        jax.ShapeDtypeStruct((T, 2, 512), BF),
        jax.ShapeDtypeStruct((2, HD), F32),
    ]
    out = pl.pallas_call(
        kernel,
        out_shape=shapes,
        in_specs=[anywhere] * 10,
        out_specs=[anywhere, anywhere, anywhere, vmem],
        scratch_shapes=[
            pltpu.VMEM((2, HD), F32),
            pltpu.VMEM((2, T, HD), F32),
            pltpu.VMEM((2, HD // 2, T), F32),
            pltpu.SMEM((1, 1), jnp.int32),
            pltpu.SMEM((1, 1), jnp.int32),
            pltpu.SMEM((1,), jnp.int32),
            pltpu.VMEM((T, 4096), BF),
            pltpu.VMEM((T, 4096), BF),
            pltpu.VMEM((T, 2, 512), BF),
            pltpu.VMEM((KVH, T, 2, HD), BF),
            pltpu.VMEM((T, 2, 512), BF),
            pltpu.VMEM((T, 2, 512), BF),
            pltpu.VMEM((heads, HD, T), F32),
            pltpu.VMEM((KVH, HD, GW * T), BF),
            pltpu.VMEM((heads, 8, T), F32),
            pltpu.VMEM((heads, T, T), F32),
            pltpu.VMEM((heads, T, T), F32),
            pltpu.VMEM((heads, 8, T), F32),
            pltpu.VMEM((heads, 8, T), F32),
            pltpu.VMEM((KVH, T, GW * T), BF),
            pltpu.VMEM((KVH, 2 * T, HD), BF),
            pltpu.VMEM((KVH, 2 * T, HD), BF),
            pltpu.VMEM((KVH, HD, 2 * T), BF),
            pltpu.VMEM((KVH, T, HD), F32),
            pltpu.VMEM((KVH, T, HD), F32),
            pltpu.VMEM((4, HD // 2, T), F32),
            pltpu.VMEM((8, T), F32),
            pltpu.VMEM((8, T), F32),
            pltpu.VMEM((T, HD), F32),
            pltpu.VMEM((T, HD), F32),
            pltpu.VMEM((T, HD), F32),
            pltpu.VMEM((HD, T), F32),
            pltpu.VMEM((8, HD), F32),
            pltpu.VMEM((GW, T, T), F32),
            pltpu.VMEM((GW, T, T), F32),
            pltpu.VMEM((T, GW * T), BF),
            pltpu.VMEM((KVH, 2 * T, GW * T), BF),
            [pltpu.VMEM((NX, CH, 2, HD), BF)] * KVH,
            [pltpu.VMEM((2, CH, 2, HD), BF)] * KVH,
            pltpu.VMEM((KVH, T, 2, HD), BF),
            pltpu.VMEM((KVH, T, 2 * HD), BF),
            pltpu.VMEM((KVH, NX, CH, 2 * HD), BF),
            pltpu.VMEM((KVH, CH, 2 * HD), BF),
            pltpu.VMEM((KVH, CH, 2 * HD), BF),
            pltpu.VMEM((KVH, CH, 2 * HD), F32),
            pltpu.VMEM((KVH, T, 2 * HD), BF),
            pltpu.VMEM((8, 8, HD), F32),
            pltpu.VMEM((16, 8, HD), F32),
            pltpu.VMEM((16, 8, HD), F32),
            dma((2, KVH)),
            dma((7,)),
            dma((6,)),
            dma((KVH,)),
            dma((2 * KVH,)),
            dma((KVH, NX)),
            dma((KVH, NX)),
            dma((KVH,)),
            dma((KVH,)),
            dma((KVH, NX)),
            dma((KVH, NX)),
            dma((KVH, NX)),
            dma((KVH, NX)),
            dma((KVH,)),
            dma((KVH,)),
            dma((KVH, NX)),
            dma((KVH, NX)),
            dma((8,)),
            dma((8,)),
            dma((16,)),
            dma((16,)),
            dma((16,)),
            dma((16,)),
        ],
        compiler_params=pltpu.CompilerParams(
            collective_id=0, has_side_effects=True, vmem_limit_bytes=56 << 20
        ),
    )(
        queries[0, 0], resp_kv[0, 0], prefix_kv[0, 0], norm_gains, dout[0, 0],
        lengths, rewards, owner, natural, transposed,
    )
    out = pl.pallas_call(
        finish,
        out_shape=shapes,
        in_specs=[anywhere] * 4,
        out_specs=[anywhere] * 4,
        scratch_shapes=[pltpu.VMEM(a.shape, a.dtype) for a in shapes] + [dma((7,)), dma((7,))],
        compiler_params=pltpu.CompilerParams(vmem_limit_bytes=56 << 20),
    )(*out)
    return (out[0][None, None], out[1][None, None], out[2][None, None], out[3])


def solution(mesh):
    return jax.shard_map(
        body,
        mesh=mesh,
        in_specs=(
            P("prompts", "group", None, None),
            P("prompts", "group", None, None, None),
            P("prompts", "group", None, None, None),
            P(),
            P("prompts", "group", None, None),
            P("prompts", "group"),
            P("prompts", "group"),
            P("prompts"),
        ),
        out_specs=(
            P("prompts", "group", None, None),
            P("prompts", "group", None, None, None),
            P("prompts", "group", None, None, None),
            P(),
        ),
        check_vma=False,
    )
```
